128 devices in a mesh: seq: 16 (over x, y), head: 8 (over z, core).
Axes of the slice: x: 4, y: 4, z: 4, core: 2. Of those that a mesh axis runs over, the one named last changes fastest.
Arguments:
- queries: bfloat16 [16384, 4096], P(('seq', 'head')), may hold values from -6 to 6
- keys: bfloat16 [16384, 4096], P(('seq', 'head')), may hold values from -6 to 6
- values: bfloat16 [16384, 4096], P(('seq', 'head')), may hold values from -6 to 6
- beta: bfloat16 [16384, 32], P(('seq', 'head')), may hold values from 0 to 1
- log_decay: bfloat16 [16384, 32], P(('seq', 'head')), may hold values from -1 to 0
- seg_lengths: int32 [8], replicated, may hold values from 1 to 12288, 16384 in all
Outputs:
- mixed: bfloat16 [16384, 4096], P(('seq', 'head'))
The draws below stay inside these ranges and needn't reach their ends.
All inputs are finite; a program needn't handle non-finite values.
Results may differ from the reference program's by a relative error of at most 0.0017.
Values may be sent and summed in bfloat16 or wider, within the bound.
No kernel may reach another device: no remote copies, remote signals or barrier semaphores. Data moves between devices by JAX's collectives and lax.ppermute only.
A program may use at most 128 MiB of HBM per device.

```python
import math
from functools import partial
import jax
import jax.numpy as jnp
import numpy as np
from jax import lax

H = 32
DK = 128
DV = 128
SPAN = 64
NSEG = 8
TOK_DEV = 128
PACKED_TOKENS = 16384


def head_decay_slowness(key, share):
    pick = jax.random.uniform(jax.random.fold_in(key, 11), (H,))
    slow_part = jax.random.uniform(jax.random.fold_in(key, 12), (H,), minval=0.85, maxval=1.0)
    fast_part = jax.random.uniform(jax.random.fold_in(key, 13), (H,), minval=0.0, maxval=0.6)
    return jnp.where(pick < share, slow_part, fast_part)


def draw_keys(key, part):
    key = jax.random.fold_in(key, 5)
    count = PACKED_TOKENS // SPAN
    direction = jax.random.normal(jax.random.fold_in(key, 1), (count, 1, H, DK), dtype=jnp.float32)
    lean = 2.0
    noise = jax.random.normal(jax.random.fold_in(key, 2), (count, SPAN, H, DK), dtype=jnp.float32)
    rows = jnp.clip(lean * direction + noise, -6.0, 6.0)
    return rows.reshape(PACKED_TOKENS, H * DK).astype(jnp.bfloat16)


def draw_log_decay(key, part):
    share = 0.5
    slowness = head_decay_slowness(key, share)
    log_rate = (1.0 - slowness) * math.log(1.0 / 40.0) + slowness * math.log(0.5 / PACKED_TOKENS)
    rough = jax.random.uniform(jax.random.fold_in(key, 21), (PACKED_TOKENS, H), minval=-0.7, maxval=0.7)
    blocky = jax.random.uniform(jax.random.fold_in(key, 22), (PACKED_TOKENS // TOK_DEV, H), minval=-0.7, maxval=0.7)
    blocky = jnp.repeat(blocky, TOK_DEV, axis=0)
    rate = jnp.exp(log_rate[None, :] + rough + blocky)
    segment_start_flags = jax.random.randint(jax.random.fold_in(key, 23), (8,), 0, PACKED_TOKENS)
    reset_hit_mask = jnp.any(jnp.arange(PACKED_TOKENS)[:, None] == segment_start_flags[None, :], axis=1)
    loss = jax.random.uniform(jax.random.fold_in(key, 24), (PACKED_TOKENS, H), minval=math.log(0.5), maxval=math.log(0.8))
    return (-rate + jnp.where(reset_hit_mask[:, None], loss, 0.0)).astype(jnp.bfloat16)


def draw_beta(key, part):
    share = 0.5
    slowness = head_decay_slowness(key, share)
    log_base = (1.0 - slowness) * math.log(0.5) + slowness * math.log(min(64.0 / PACKED_TOKENS, 0.5))
    rough = jax.random.uniform(jax.random.fold_in(key, 31), (PACKED_TOKENS, H), minval=-0.6, maxval=0.6)
    return jnp.exp(log_base[None, :] + rough).astype(jnp.bfloat16)


def levels(own_key, dims, cuts, low, high):
    factor_of = 1.0
    for position, shards_of in cuts:
        steps = jax.random.uniform(jax.random.fold_in(jax.random.fold_in(own_key, 6), position), (shards_of,), jnp.float32, low / len(cuts), high / len(cuts))
        factor_of = factor_of * jnp.repeat(jnp.exp(steps), dims[position] // shards_of).reshape((-1,) + (1,) * (len(dims) - 1 - position))
    return factor_of


def split_up(count, total, limit, skew):
    portions = [(1 << 20) // math.isqrt(grade ** skew) + 1 for grade in range(2, count + 1)]
    spare, counts = total - limit - (count - 1), [1] * (count - 1)
    while spare > 0:
        candidates = [i for i in range(count - 1) if counts[i] < limit]
        whole, remaining = sum([portions[i] for i in candidates]), spare
        for i in candidates:
            addition = min(limit - counts[i], max(1, remaining * portions[i] // whole), spare)
            counts[i] = counts[i] + addition
            spare = spare - addition
    return np.array([limit] + counts)


def ragged_sizes(stream_key, count, total, reach, slope):
    if count == 2:
        one = jax.random.randint(stream_key, (), max(1, total - reach), min(reach, total - 1) + 1)
        return jnp.stack([one, total - one])
    lengths = jnp.asarray(split_up(count, total, reach, slope), jnp.int32)
    twos = (count - 1) // 2
    source_of, receiver = lengths[1:1 + 2 * twos:2], lengths[2:2 + 2 * twos:2]
    room = jnp.minimum(source_of - 1, reach - receiver)
    moved = jax.random.randint(jax.random.fold_in(stream_key, 1), (twos,), 0, 1 << 20) % (room + 1)
    lengths = lengths.at[1:1 + 2 * twos:2].set(source_of - moved).at[2:2 + 2 * twos:2].set(receiver + moved)
    return lengths[jax.random.permutation(jax.random.fold_in(stream_key, 2), count)]


def normal_values(rng, shape, scale, reach, shards=(), kind=jnp.bfloat16):
    values = jax.random.normal(rng, shape, jnp.float32) * scale
    if len(shards) > 0:
        values = levels(rng, shape, shards, -0.22, 0.18) * values
    return jnp.clip(values, min=-reach, max=reach).astype(kind)


def setup_inputs(seed: int = 0) -> dict:
    splits = jax.random.split(jax.random.key(seed), 7)
    queries = normal_values(splits[0], (PACKED_TOKENS, H * DK), 1.0, 6.0, ((0, 128),))
    keys = draw_keys(jax.random.fold_in(splits[6], 71), 0)
    values = normal_values(splits[2], (PACKED_TOKENS, H * DV), 1.0, 6.0, ((0, 128),))
    beta = draw_beta(jax.random.fold_in(splits[6], 71), 0)
    log_decay = draw_log_decay(jax.random.fold_in(splits[6], 71), 0)
    seg_lengths = ragged_sizes(splits[5], NSEG, PACKED_TOKENS, PACKED_TOKENS * 3 // 4, 2).astype(jnp.int32)
    return dict(queries=queries, keys=keys, values=values, beta=beta, log_decay=log_decay, seg_lengths=seg_lengths)


def span_parts(query_rows, key_rows, value_rows, write_rate, log_gate, reset_flags, inclusive):
    highest = lax.Precision.HIGHEST
    block_rows = query_rows.shape[0]
    log_level = jnp.cumsum(log_gate)
    region = jnp.cumsum(reset_flags)
    row_indices = jnp.arange(block_rows)[:, None]
    col_ids = jnp.arange(block_rows)[None, :]
    inside_segment_mask = (col_ids <= row_indices) & (region[:, None] == region[None, :])
    log_gap = jnp.where(inside_segment_mask, log_level[:, None] - log_level[None, :], 0.0)
    weight = jnp.where(inside_segment_mask, jnp.exp(log_gap), 0.0)
    carried = jnp.where(region == 0, jnp.exp(log_level), 0.0)
    strictly = col_ids < row_indices
    intersection = jnp.dot(key_rows, key_rows.T, precision=highest)
    system = jnp.eye(block_rows, dtype=query_rows.dtype) + jnp.where(strictly, write_rate[:, None] * weight * intersection, 0.0)
    right_side = jnp.concatenate([write_rate[:, None] * value_rows, (write_rate * carried)[:, None] * key_rows], axis=1)
    solved = lax.linalg.triangular_solve(system, right_side, left_side=True, lower=True, unit_diagonal=True)
    value_width = value_rows.shape[1]
    update = solved[:, :value_width]
    shrink = solved[:, value_width:]
    scores = jnp.dot(query_rows, key_rows.T, precision=highest) * weight
    if not inclusive:
        scores = jnp.where(strictly, scores, 0.0)
    local_out = jnp.dot(scores, update, precision=highest)
    effective = carried[:, None] * query_rows - jnp.dot(scores, shrink, precision=highest)
    trailing_weight = weight[block_rows - 1]
    scaled = trailing_weight[:, None] * key_rows
    transit = carried[block_rows - 1] * jnp.eye(key_rows.shape[1], dtype=query_rows.dtype) - jnp.dot(shrink.T, scaled, precision=highest)
    inject = jnp.dot(update.T, scaled, precision=highest)
    return (local_out, effective, transit, inject)

def block_pieces(query_rows, key_rows, value_rows, write_rate, log_gate, reset_flags, inclusive):
    count = query_rows.shape[0] // SPAN

    def split(member):
        return member.reshape((count, SPAN) + member.shape[1:])
    return jax.vmap(partial(span_parts, inclusive=inclusive))(split(query_rows), split(key_rows), split(value_rows), split(write_rate), split(log_gate), split(reset_flags))

def run_direction(query_rows, key_rows, value_rows, write_rate, log_gate, reset_flags, inclusive):
    highest = lax.Precision.HIGHEST
    pieces = block_pieces(query_rows, key_rows, value_rows, write_rate, log_gate, reset_flags, inclusive)
    start = jnp.zeros((value_rows.shape[1], key_rows.shape[1]), query_rows.dtype)

    def advance(state, piece):
        out_block, effect_rows, transit_step, inject_step = piece
        produced = out_block + jnp.dot(effect_rows, state.T, precision=highest)
        return (jnp.dot(state, transit_step, precision=highest) + inject_step, produced)
    final_state, outputs = lax.scan(advance, start, pieces)
    return outputs.reshape(-1, value_rows.shape[1])

def reference(queries, keys, values, beta, log_decay, seg_lengths):
    total = queries.shape[0]
    starts = (jnp.cumsum(seg_lengths) - seg_lengths).astype(jnp.int32)
    positions = jnp.arange(total, dtype=jnp.int32)
    forward_reset = jnp.any(positions[:, None] == starts[None, :], axis=1).astype(jnp.int32)
    backward_reset = (jnp.any((positions + 1)[:, None] == starts[None, :], axis=1) | (positions == total - 1)).astype(jnp.int32)

    def by_head(array, width):
        return array.reshape(total, H, width).transpose(1, 0, 2)
    head_data = (by_head(queries, DK), by_head(keys, DK), by_head(values, DV), beta.T, log_decay.T)

    def one_head(member):
        query_rows = member[0].astype(jnp.float32)
        key_raw = member[1].astype(jnp.float32)
        value_rows = member[2].astype(jnp.float32)
        write_rate = member[3].astype(jnp.float32)
        log_gate = member[4].astype(jnp.float32)
        key_rows = key_raw / jnp.sqrt(lax.optimization_barrier(jnp.sum(key_raw * key_raw, axis=-1, keepdims=True)) + 1e-06)
        forward = run_direction(query_rows, key_rows, value_rows, write_rate, log_gate, forward_reset, True)
        backward = run_direction(query_rows[::-1], key_rows[::-1], value_rows[::-1], write_rate[::-1], log_gate[::-1], backward_reset[::-1], False)[::-1]
        return forward + backward
    outputs = lax.map(one_head, head_data)
    return outputs.transpose(1, 0, 2).reshape(total, H * DV).astype(jnp.bfloat16)
```

```python
import functools

import jax
import jax.numpy as jnp
from jax import lax
from jax.experimental import pallas as pl
from jax.experimental.pallas import tpu as pltpu
from jax.sharding import Mesh, PartitionSpec as P

D = 128
C = 128
BASE = 32
EXTRA = 16
CUT = 128.0
F32 = jnp.float32
BF16 = jnp.bfloat16
GROUP = ("y", "z", "core")


def split(x):
    hi = x.astype(BF16)
    return hi, (x - hi.astype(F32)).astype(BF16)


def mm(a, b):
    return lax.dot_general(a, b, (((1,), (0,)), ((), ())), preferred_element_type=F32)


def mm_t(a, b):
    return lax.dot_general(a, b, (((1,), (1,)), ((), ())), preferred_element_type=F32)


def lhs3(pair):
    return jnp.concatenate([pair[0], pair[1], pair[0]], axis=1)


def rhs3(pair):
    return jnp.concatenate([pair[0], pair[0], pair[1]], axis=0)


def rhs3_t(pair):
    return jnp.concatenate([pair[0], pair[0], pair[1]], axis=1)


def dot3(a, b):
    return mm(lhs3(split(a)), rhs3(split(b)))


def dot_exact_rhs(a, b):
    return mm(jnp.concatenate(split(a), axis=1), jnp.concatenate([b, b], axis=0))


def iota(shape, dim):
    return lax.broadcasted_iota(jnp.int32, shape, dim)


def key_kernel(units, starts_ref, base_ref, kmsg_ref, a_hi, a_lo, w_ref, wg_ref, x_ref, y_ref, yt_ref, se_ref, rows_ref):
    step = pl.program_id(0)
    row, col = iota((C, C), 0), iota((C, C), 1)
    extra = kmsg_ref[:, C : C + EXTRA, :].astype(F32)
    beta = jnp.concatenate([extra[u, 0:1] for u in range(units)], axis=0)
    logd = jnp.concatenate([extra[u, 1:2] for u in range(units)], axis=0)
    level = mm(logd.astype(BF16), (row <= col).astype(BF16))
    begin = base_ref[0] + (step * units + iota((units, C), 0)) * C
    place = begin + iota((units, C), 1)
    cuts = jnp.zeros((units, C), F32)
    for n in range(starts_ref.shape[0]):
        at = starts_ref[n]
        cuts += jnp.where((begin < at) & (at <= place), 1.0, 0.0)
    level = level - CUT * cuts
    last = level[:, C - 1 : C]
    carried = jnp.exp(level)
    trail = jnp.exp(last - level)
    gate = jnp.exp(logd)
    inverse_gate = jnp.exp(-logd)
    eye = row == col
    keys = [kmsg_ref[u, :C, :] for u in range(units)]
    gram = [mm_t(k, k) for k in keys]
    norm = jnp.concatenate(
        [jnp.sum(jnp.where(eye, g, 0.0), axis=0, keepdims=True) for g in gram], axis=0
    )
    scale = 1.0 / jnp.sqrt(norm + 1e-6)
    columns = jnp.concatenate(
        [level, beta * scale, beta, carried * scale, inverse_gate], axis=0
    ).T

    def column(which, u):
        return columns[:, which * units + u : which * units + u + 1]

    same = (row // BASE) == (col // BASE)
    systems, compact = [], []
    for u in range(units):
        decay = jnp.exp(-jnp.abs(column(0, u) - level[u : u + 1]))
        weighted = decay * scale[u : u + 1]
        se_ref[u] = weighted
        system = jnp.where(row > col, gram[u] * weighted * column(1, u), 0.0)
        systems.append(system)
        inside = jnp.where(same, system, 0.0)
        compact.append(sum(inside[i * BASE : (i + 1) * BASE] for i in range(C // BASE)))
    lane = iota((BASE, C), 1)
    small_row = iota((BASE, C), 0)
    solved = [jnp.where(small_row == lane % BASE, 1.0, 0.0) for u in range(units)]
    first = (lane // BASE) * BASE
    for j in range(BASE - 1):
        top = (j // 8) * 8
        for u in range(units):
            factor = jnp.take_along_axis(compact[u][top:], first[top:] + j, axis=1)
            low = solved[u][top:] - factor * solved[u][j : j + 1]
            solved[u] = jnp.concatenate([solved[u][:top], low], axis=0) if top else low
    zero32 = jnp.zeros((BASE, C), F32)
    zero64 = jnp.zeros((2 * BASE, C), F32)
    full = [
        jnp.where(same, jnp.concatenate([solved[u]] * (C // BASE), axis=0), 0.0)
        for u in range(units)
    ]
    wide = iota((BASE, C), 1)
    part = []
    for u in range(units):
        left = jnp.concatenate(
            [
                jnp.where(wide < 32, systems[u][32:64], 0.0),
                jnp.where((wide >= 64) & (wide < 96), systems[u][96:128], 0.0),
            ],
            axis=0,
        )
        part.append(dot3(left, full[u]))
    for u in range(units):
        spread = jnp.concatenate([zero32, part[u][:32], zero32, part[u][32:]], axis=0)
        t = full[u]
        delta = dot3(jnp.concatenate([t[32:64], t[96:128]], axis=0), spread)
        full[u] = jnp.concatenate(
            [t[:32], t[32:64] - delta[:32], t[64:96], t[96:] - delta[32:]], axis=0
        )
    wide = iota((2 * BASE, C), 1)
    for u in range(units):
        part[u] = dot3(jnp.where(wide < 64, systems[u][64:], 0.0), full[u])
    for u in range(units):
        t = full[u]
        delta = dot3(t[64:], jnp.concatenate([zero64, part[u]], axis=0))
        full[u] = jnp.concatenate([t[:64], t[64:] - delta], axis=0)
    for u in range(units):
        one = slice(u, u + 1)
        y = full[u] * beta[one]
        y_ref[u] = y
        w = dot_exact_rhs(y * (scale[one] * carried[one]), keys[u])
        w_ref[u] = w
        wg_ref[u] = w * column(4, u)
        yt = full[u].T * column(2, u)
        yt_ref[u] = yt * inverse_gate[one]
        x = dot_exact_rhs(yt * (trail[one] * scale[one]), keys[u])
        x_ref[u] = x
        kt = keys[u].T
        back = jnp.concatenate(split(x * column(3, u)), axis=0)
        a = jnp.where(eye, carried[one, C - 1 : C], 0.0) - mm(jnp.concatenate([kt, kt], axis=1), back)
        hi, lo = split(a)
        a_hi[u] = hi
        a_lo[u] = lo
        rows_ref[u] = jnp.concatenate(
            [carried[one], trail[one], gate[one], jnp.zeros((5, C), F32)], axis=0
        )


def is_start(starts_ref, at):
    found = starts_ref[0] == at
    for n in range(1, starts_ref.shape[0]):
        found = found | (starts_ref[n] == at)
    return found


def scan_kernel(
    units, chunks, starts_ref, base_ref,
    af_hi, af_lo, vf_ref, x_ref, ab_hi, ab_lo, vb_ref, wg_ref, y_ref, yt_ref,
    zf_hi, zf_lo, zb_hi, zb_lo, uf_ref, ub_ref, total_ref, forward, backward,
):
    step = pl.program_id(0)

    @pl.when(step == 0)
    def _():
        start = jnp.concatenate(
            [jnp.zeros((D, D), F32), jnp.where(iota((D, D), 0) == iota((D, D), 1), 1.0, 0.0)],
            axis=0,
        )
        forward[...] = start
        backward[...] = start

    zf, zb = forward[...], backward[...]
    zero = jnp.zeros((D, D), F32)
    for u in range(units):
        n = step * units + u
        r = units - 1 - u
        m = chunks - 1 - n
        vt = vf_ref[u].T
        inject = mm(jnp.concatenate([vt, vt], axis=1), jnp.concatenate(split(x_ref[u]), axis=0))
        cut = is_start(starts_ref, base_ref[0] + n * C) & (n > 0)
        zf = zf * jnp.where(cut, 0.0, 1.0)
        pair = split(zf)
        zf_hi[u] = pair[0]
        zf_lo[u] = pair[1]
        zf = mm(lhs3(pair), rhs3((af_hi[u], af_lo[u]))) + jnp.concatenate([inject, zero], axis=0)
        vt = vb_ref[r].T
        inject = mm(jnp.concatenate([vt, vt], axis=1), jnp.concatenate(split(wg_ref[r]), axis=0))
        cut = is_start(starts_ref, base_ref[0] + (m + 1) * C) & (n > 0)
        zb = zb * jnp.where(cut, 0.0, 1.0)
        pair = split(zb)
        zb_hi[r] = pair[0]
        zb_lo[r] = pair[1]
        zb = mm_t(lhs3(pair), rhs3_t((ab_hi[r], ab_lo[r]))) + jnp.concatenate([inject, zero], axis=0)
        uf_ref[u] = dot_exact_rhs(y_ref[u], vf_ref[u])
        ub_ref[u] = dot_exact_rhs(yt_ref[u], vf_ref[u])
    forward[...] = zf
    backward[...] = zb
    total_ref[0] = zf[D:]
    total_ref[1] = zf[:D]
    total_ref[2] = zb[:D]


def query_kernel(units, q_ref, k_ref, se_ref, w_ref, x_ref, uf_ref, ub_ref, rows_ref, zf_hi, zf_lo, zb_hi, zb_lo, out_ref, f_ref):
    row, col = iota((C, C), 0), iota((C, C), 1)
    for u in range(units):
        q = q_ref[u]
        columns = rows_ref[u].T
        carried, trail, gate = columns[:, 0:1], columns[:, 1:2], columns[:, 2:3]
        scores = mm_t(q, k_ref[u]) * se_ref[u]
        lower = split(jnp.where(col <= row, scores, 0.0))
        upper = split(jnp.where(col > row, scores, 0.0))
        first = mm(lhs3(lower), rhs3(split(jnp.concatenate([uf_ref[u], w_ref[u]], axis=1))))
        second = mm(lhs3(upper), rhs3(split(jnp.concatenate([ub_ref[u], x_ref[u]], axis=1))))
        q = q.astype(F32)
        effect_f = carried * q - first[:, D:]
        effect_b = gate * (trail * q - second[:, D:])
        third = mm_t(lhs3(split(effect_f)), rhs3_t((zf_hi[u], zf_lo[u])))
        fourth = mm_t(lhs3(split(effect_b)), rhs3_t((zb_hi[u], zb_lo[u])))
        out_ref[u] = first[:, :D] + gate * second[:, :D] + third[:, :D] + fourth[:, :D]
        f_ref[u] = jnp.concatenate([third[:, D:], fourth[:, D:]], axis=1)


def final_kernel(units, starts_ref, base_ref, span, part_ref, f_ref, one_ref, two_ref, three_ref, mixed_ref, s_hi, s_lo):
    step = pl.program_id(0)

    @pl.when(step == 0)
    def _():
        mine = base_ref[0] // span
        arrived = {1: one_ref, 2: two_ref, 3: three_ref}
        sf = jnp.zeros((D, D), F32)
        for d in (3, 2, 1):
            cut = is_start(starts_ref, (mine - d) * span)
            moved = dot3(sf * jnp.where(cut, 0.0, 1.0), arrived[d][0]) + arrived[d][1]
            sf = jnp.where(d <= mine, moved, sf)
        sf = sf * jnp.where(is_start(starts_ref, mine * span), 0.0, 1.0)
        sb = jnp.zeros((D, D), F32)
        for d in (1, 2, 3):
            cut = is_start(starts_ref, (mine - d + 5) * span)
            moved = mm_t(
                lhs3(split(sb * jnp.where(cut, 0.0, 1.0))), rhs3_t(split(arrived[d][0]))
            ) + arrived[d][2]
            sb = jnp.where(d > mine, moved, sb)
        sb = sb * jnp.where(is_start(starts_ref, (mine + 1) * span), 0.0, 1.0)
        hi, lo = split(jnp.concatenate([sf, sb], axis=1))
        s_hi[...] = hi
        s_lo[...] = lo

    state = rhs3_t((s_hi[...], s_lo[...]))
    for u in range(units):
        mixed_ref[u] = (part_ref[u] + mm_t(lhs3(split(f_ref[u])), state)).astype(BF16)


def blocks(units, *tail, flip=None):
    if flip is None:
        return pl.BlockSpec((units,) + tail, lambda i: (i,) + (0,) * len(tail))
    return pl.BlockSpec((units,) + tail, lambda i: (flip - 1 - i,) + (0,) * len(tail))


SCALARS = [pl.BlockSpec(memory_space=pltpu.SMEM)] * 2


def params():
    return pltpu.CompilerParams(vmem_limit_bytes=48 * 1024 * 1024)


def cost(flops, moved):
    return pl.CostEstimate(flops=flops, bytes_accessed=moved, transcendentals=0)


def on_device(queries, keys, values, beta, log_decay, seg_lengths):
    own, width = queries.shape
    heads = width // D
    x = lax.axis_index("x")
    groups = lax.axis_size("x")
    chunks = heads
    span = chunks * C
    order = jnp.arange(seg_lengths.shape[0])
    starts = jnp.sum(jnp.where(order[None, :] < order[:, None], seg_lengths[None, :], 0), axis=1)
    starts = starts.astype(jnp.int32)
    base = (x * span).astype(jnp.int32).reshape(1)

    def by_head(array):
        return array.reshape(own, heads, D).transpose(1, 0, 2)

    def spread(array):
        return lax.all_to_all(array, GROUP, split_axis=0, concat_axis=0, tiled=True)

    extra = jnp.stack([beta.T, log_decay.T], axis=1)
    extra = jnp.concatenate([extra, jnp.zeros((heads, EXTRA - 2, C), BF16)], axis=1)
    kmsg = spread(jnp.concatenate([by_head(keys), extra], axis=1))
    v = spread(by_head(values))
    q = spread(by_head(queries))

    def out(*shape, dtype=F32):
        return jax.ShapeDtypeStruct((chunks,) + shape, dtype)

    units = 8
    a_hi, a_lo, w, wg, xx, y, yt, se, rows = pl.pallas_call(
        functools.partial(key_kernel, units),
        grid=(chunks // units,),
        in_specs=SCALARS + [blocks(units, C + EXTRA, D)],
        out_specs=[blocks(units, C, D)] * 8 + [blocks(units, 8, C)],
        out_shape=[out(C, D, dtype=BF16)] * 2 + [out(C, D)] * 6 + [out(8, C)],
        compiler_params=params(),
        cost_estimate=cost(20_000_000_000, 20_000_000),
        name="key_maps",
    )(starts, base, kmsg)
    n = chunks // units
    zf_hi, zf_lo, zb_hi, zb_lo, uf, ub, total = pl.pallas_call(
        functools.partial(scan_kernel, units, chunks),
        grid=(n,),
        in_specs=SCALARS
        + [blocks(units, C, D)] * 4
        + [blocks(units, C, D, flip=n)] * 4
        + [blocks(units, C, D)] * 2,
        out_specs=[blocks(units, 2 * C, D)] * 2
        + [blocks(units, 2 * C, D, flip=n)] * 2
        + [blocks(units, C, D)] * 2
        + [pl.BlockSpec((3, D, D), lambda i: (0, 0, 0))],
        out_shape=[out(2 * C, D, dtype=BF16)] * 4
        + [out(C, D)] * 2
        + [jax.ShapeDtypeStruct((3, D, D), F32)],
        scratch_shapes=[pltpu.VMEM((2 * D, D), F32)] * 2,
        compiler_params=params(),
        cost_estimate=cost(20_000_000_000, 20_000_000),
        name="scan",
    )(starts, base, a_hi, a_lo, v, xx, a_hi, a_lo, v, wg, y, yt)
    arrived = [
        lax.ppermute(total, "x", [(i, (i + d) % groups) for i in range(groups)]) for d in (1, 2, 3)
    ]
    part, f = pl.pallas_call(
        functools.partial(query_kernel, units),
        grid=(n,),
        in_specs=[blocks(units, C, D)] * 7
        + [blocks(units, 8, C)]
        + [blocks(units, 2 * C, D)] * 4,
        out_specs=[blocks(units, C, D), blocks(units, C, 2 * D)],
        out_shape=[out(C, D), out(C, 2 * D)],
        compiler_params=params(),
        cost_estimate=cost(20_000_000_000, 20_000_000),
        name="local_out",
    )(q, kmsg[:, :C, :], se, w, xx, uf, ub, rows, zf_hi, zf_lo, zb_hi, zb_lo)

    whole = pl.BlockSpec((3, D, D), lambda i: (0, 0, 0))

    def final(starts_ref, base_ref, *refs):
        final_kernel(units, starts_ref, base_ref, span, *refs)

    mixed = pl.pallas_call(
        final,
        grid=(n,),
        in_specs=SCALARS + [blocks(units, C, D), blocks(units, C, 2 * D)] + [whole] * 3,
        out_specs=blocks(units, C, D),
        out_shape=out(C, D, dtype=BF16),
        scratch_shapes=[pltpu.VMEM((D, 2 * D), BF16)] * 2,
        compiler_params=params(),
        cost_estimate=cost(2_000_000_000, 10_000_000),
        name="final",
    )(starts, base, part, f, *arrived)
    back = spread(mixed)
    return back.transpose(1, 0, 2).reshape(own, width)


def solution(mesh):
    fine = Mesh(mesh.devices.reshape(4, 4, 4, 2), ("x", "y", "z", "core"))
    rows = P(("x", "y", "z", "core"), None)
    return jax.shard_map(
        on_device,
        mesh=fine,
        in_specs=(rows,) * 5 + (P(),),
        out_specs=rows,
        check_vma=False,
    )
```

```python
import functools

import jax
import jax.numpy as jnp
from jax import lax
from jax.experimental import pallas as pl
from jax.experimental.pallas import tpu as pltpu
from jax.sharding import Mesh, PartitionSpec as P

D = 128
C = 128
BASE = 32
EXTRA = 16
CUT = 128.0
VMEM_MIB = 50
F32 = jnp.float32
BF16 = jnp.bfloat16
GROUP = ("y", "z", "core")


def split(x):
    hi = x.astype(BF16)
    return hi, (x - hi.astype(F32)).astype(BF16)


def mm(a, b):
    return lax.dot_general(a, b, (((1,), (0,)), ((), ())), preferred_element_type=F32)


def lhs3(pair):
    return jnp.concatenate([pair[0], pair[1], pair[0]], axis=1)


def rhs3(pair):
    return jnp.concatenate([pair[0], pair[0], pair[1]], axis=0)


def dot3(a, b):
    return mm(lhs3(split(a)), rhs3(split(b)))


def beside(x):
    return jnp.concatenate(split(x), axis=1)


def below(x):
    return jnp.concatenate(split(x), axis=0)


def twice(b, axis):
    return jnp.concatenate([b, b], axis=axis)


def widen(ab):
    return jnp.concatenate([ab, ab[:, : ab.shape[1] // 2]], axis=1)


def halves(ab):
    return ab[:, : ab.shape[1] // 2], ab[:, ab.shape[1] // 2 :]


def deepen(hi, lo):
    return jnp.concatenate([hi, hi, lo], axis=0)


def iota(shape, dim):
    return lax.broadcasted_iota(jnp.int32, shape, dim)


def key_kernel(units, starts_ref, base_ref, kmsg_ref, maps_ref, kt_ref, rows_ref):
    step = pl.program_id(0)
    row, col = iota((C, C), 0), iota((C, C), 1)
    extra = kmsg_ref[:, C : C + EXTRA, :].astype(F32)
    beta = jnp.concatenate([extra[u, 0:1] for u in range(units)], axis=0)
    logd = jnp.concatenate([extra[u, 1:2] for u in range(units)], axis=0)
    level = mm(logd.astype(BF16), (row <= col).astype(BF16))
    begin = base_ref[0] + (step * units + iota((units, C), 0)) * C
    place = begin + iota((units, C), 1)
    cuts = jnp.zeros((units, C), F32)
    for n in range(starts_ref.shape[0]):
        at = starts_ref[n]
        cuts += jnp.where((begin < at) & (at <= place), 1.0, 0.0)
    level = level - CUT * cuts
    last = level[:, C - 1 : C]
    carried = jnp.exp(level)
    trail = jnp.exp(last - level)
    gate = jnp.exp(logd)
    inverse_gate = jnp.exp(-logd)
    eye = row == col
    keys = [kmsg_ref[u, :C, :] for u in range(units)]
    turned = [k.T for k in keys]
    gram = [mm(keys[u], turned[u]) for u in range(units)]
    norm = jnp.concatenate(
        [jnp.sum(jnp.where(eye, g, 0.0), axis=0, keepdims=True) for g in gram], axis=0
    )
    scale = 1.0 / jnp.sqrt(norm + 1e-6)
    columns = jnp.concatenate(
        [level, beta * scale, beta, carried * scale, trail * scale], axis=0
    ).T

    def column(which, u):
        return columns[:, which * units + u : which * units + u + 1]

    same = (row // BASE) == (col // BASE)
    systems, compact = [], []
    for u in range(units):
        decay = jnp.exp(-jnp.abs(column(0, u) - level[u : u + 1]))
        weighted = decay * scale[u : u + 1]
        maps_ref[u, 8] = beside(weighted)
        system = jnp.where(row > col, gram[u] * weighted * column(1, u), 0.0)
        systems.append(system)
        inside = jnp.where(same, system, 0.0)
        compact.append(sum(inside[i * BASE : (i + 1) * BASE] for i in range(C // BASE)))
    lane = iota((BASE, C), 1)
    small_row = iota((BASE, C), 0)
    solved = [jnp.where(small_row == lane % BASE, 1.0, 0.0) for u in range(units)]
    first = (lane // BASE) * BASE
    for j in range(BASE - 1):
        top = (j // 8) * 8
        for u in range(units):
            factor = jnp.take_along_axis(compact[u][top:], first[top:] + j, axis=1)
            low = solved[u][top:] - factor * solved[u][j : j + 1]
            solved[u] = jnp.concatenate([solved[u][:top], low], axis=0) if top else low
    zero32 = jnp.zeros((BASE, C), F32)
    zero64 = jnp.zeros((2 * BASE, C), F32)
    full = [
        jnp.where(same, jnp.concatenate([solved[u]] * (C // BASE), axis=0), 0.0)
        for u in range(units)
    ]
    wide = iota((BASE, C), 1)
    part = []
    for u in range(units):
        left = jnp.concatenate(
            [
                jnp.where(wide < 32, systems[u][32:64], 0.0),
                jnp.where((wide >= 64) & (wide < 96), systems[u][96:128], 0.0),
            ],
            axis=0,
        )
        part.append(dot3(left, full[u]))
    for u in range(units):
        spread = jnp.concatenate([zero32, part[u][:32], zero32, part[u][32:]], axis=0)
        t = full[u]
        delta = dot3(jnp.concatenate([t[32:64], t[96:128]], axis=0), spread)
        full[u] = jnp.concatenate(
            [t[:32], t[32:64] - delta[:32], t[64:96], t[96:] - delta[32:]], axis=0
        )
    wide = iota((2 * BASE, C), 1)
    for u in range(units):
        part[u] = dot3(jnp.where(wide < 64, systems[u][64:], 0.0), full[u])
    for u in range(units):
        t = full[u]
        delta = dot3(t[64:], jnp.concatenate([zero64, part[u]], axis=0))
        full[u] = jnp.concatenate([t[:64], t[64:] - delta], axis=0)
    both = [None] * units
    for u in range(units):
        one = slice(u, u + 1)
        kt_ref[u] = turned[u]
        y = full[u] * beta[one]
        yt = full[u].T * column(2, u)
        maps_ref[u, 2] = beside(y)
        maps_ref[u, 5] = beside(yt * inverse_gate[one])
        right = jnp.concatenate([y * column(4, u), yt * column(3, u)], axis=1)
        both[u] = mm(twice(turned[u], 1), below(right))
    rests = [None] * units
    for u in range(units):
        one = slice(u, u + 1)
        xt, wt = both[u][:, :C], both[u][:, C:]
        rests[u] = mm(beside(xt * (carried[one] * scale[one])), twice(keys[u], 0))
        maps_ref[u, 1] = beside(xt)
        maps_ref[u, 4] = beside(wt * inverse_gate[one])
        maps_ref[u, 6] = beside(wt.T)
        maps_ref[u, 7] = beside(xt.T)
        rows_ref[u] = jnp.concatenate(
            [carried[one], trail[one], gate[one], jnp.zeros((5, C), F32)], axis=0
        )
    for u in range(units):
        at = jnp.where(eye, carried[u : u + 1, C - 1 : C], 0.0) - rests[u]
        maps_ref[u, 0] = beside(at)
        maps_ref[u, 3] = beside(at.T)


def is_start(starts_ref, at):
    found = starts_ref[0] == at
    for n in range(1, starts_ref.shape[0]):
        found = found | (starts_ref[n] == at)
    return found


def keep(cut):
    return jnp.where(cut, 0.0, 1.0)


def scan_kernel(
    units, chunks, starts_ref, base_ref, ff_ref, vf_ref, bb_ref, vb_ref,
    zf_ref, zb_ref, total_ref, forward, backward,
):
    step = pl.program_id(0)

    @pl.when(step == 0)
    def _():
        eye = jnp.where(iota((D, D), 0) == iota((D, D), 1), 1.0, 0.0)
        start = jnp.concatenate([jnp.zeros((D, D), F32), eye], axis=1)
        forward[...] = start
        backward[...] = start

    zero = jnp.zeros((D, D), F32)

    def prepare(maps_ref, v_ref, z_ref, u):
        v2 = twice(v_ref[u], 0)
        z_ref[u, 2] = beside(mm(maps_ref[u, 2], v2))
        return mm(maps_ref[u, 1], v2)

    def advance(z, cut, inject, maps_ref, z_ref, u):
        hi, lo = split(z * keep(cut))
        z_ref[u, 0] = hi
        z_ref[u, 1] = lo
        moved = mm(widen(maps_ref[u, 0]), deepen(hi, lo))
        return moved + jnp.concatenate([inject, zero], axis=1)

    inject_f = [prepare(ff_ref, vf_ref, zf_ref, u) for u in range(units)]
    inject_b = [prepare(bb_ref, vb_ref, zb_ref, u) for u in range(units)]
    zf, zb = forward[...], backward[...]
    for u in range(units):
        r = units - 1 - u
        n = step * units + u
        m = chunks - 1 - n
        cut_f = is_start(starts_ref, base_ref[0] + n * C) & (n > 0)
        cut_b = is_start(starts_ref, base_ref[0] + (m + 1) * C) & (n > 0)
        zf = advance(zf, cut_f, inject_f[u], ff_ref, zf_ref, u)
        zb = advance(zb, cut_b, inject_b[r], bb_ref, zb_ref, r)
    forward[...] = zf
    backward[...] = zb
    total_ref[0] = zf[:, D:]
    total_ref[1] = zf[:, :D]
    total_ref[2] = zb[:, :D]


def query_kernel(units, q_ref, kt_ref, maps_ref, rows_ref, zf_ref, zb_ref, f_ref):
    row, col = iota((C, C), 0), iota((C, C), 1)

    def pairs(one, two):
        one_hi, one_lo = halves(one)
        two_hi, two_lo = halves(two)
        return deepen(
            jnp.concatenate([one_hi, two_hi], axis=1), jnp.concatenate([one_lo, two_lo], axis=1)
        )

    every = range(units)
    columns = [rows_ref[u].T for u in every]
    scores = [mm(q_ref[u], kt_ref[u]) for u in every]
    first, second = [None] * units, [None] * units
    for u in every:
        se_hi, se_lo = halves(maps_ref[u, 2])
        score = scores[u] * (se_hi.astype(F32) + se_lo.astype(F32))
        lower = beside(jnp.where(col <= row, score, 0.0))
        upper = beside(jnp.where(col > row, score, 0.0))
        first[u] = mm(widen(lower), pairs(zf_ref[u, 2], maps_ref[u, 0]))
        second[u] = mm(widen(upper), pairs(zb_ref[u, 2], maps_ref[u, 1]))
    third, fourth = [None] * units, [None] * units
    for u in every:
        carried, trail, gate = (columns[u][:, i : i + 1] for i in range(3))
        q = q_ref[u].astype(F32)
        effect_f = carried * q - first[u][:, D:]
        effect_b = gate * (trail * q - second[u][:, D:])
        third[u] = mm(widen(beside(effect_f)), deepen(zf_ref[u, 0], zf_ref[u, 1]))
        fourth[u] = mm(widen(beside(effect_b)), deepen(zb_ref[u, 0], zb_ref[u, 1]))
    for u in every:
        gate = columns[u][:, 2:3]
        total = first[u][:, :D] + gate * second[u][:, :D] + third[u][:, :D] + fourth[u][:, :D]
        f_ref[u, 0] = beside(total)
        hi, lo = split(jnp.concatenate([third[u][:, D:], fourth[u][:, D:]], axis=1))
        f_ref[u, 1] = hi
        f_ref[u, 2] = lo


def final_kernel(units, span, starts_ref, base_ref, f_ref, one_ref, two_ref, three_ref, mixed_ref, state):
    step = pl.program_id(0)

    @pl.when(step == 0)
    def _():
        mine = base_ref[0] // span
        arrived = {1: one_ref, 2: two_ref, 3: three_ref}
        turned = {d: arrived[d][0].T for d in arrived}
        sf = jnp.zeros((D, D), F32)
        sb = jnp.zeros((D, D), F32)
        for d in (1, 2, 3):
            e = 4 - d
            cut = is_start(starts_ref, (mine - e) * span)
            moved = dot3(arrived[e][0], sf * keep(cut)) + arrived[e][1]
            sf = jnp.where(e <= mine, moved, sf)
            cut = is_start(starts_ref, (mine - d + 5) * span)
            moved = dot3(turned[d], sb * keep(cut)) + arrived[d][2]
            sb = jnp.where(d > mine, moved, sb)
        sf = sf * keep(is_start(starts_ref, mine * span))
        sb = sb * keep(is_start(starts_ref, (mine + 1) * span))
        state[...] = beside(jnp.concatenate([sf, sb], axis=0))

    def rows_of(which):
        return f_ref[:, which].reshape(units * C, 2 * D)

    wide = mm(rows_of(1), state[...])
    more = mm(rows_of(2), state[:, :D])
    hi, lo = halves(rows_of(0))
    total = (hi.astype(F32) + lo.astype(F32)) + (wide[:, :D] + wide[:, D:] + more)
    mixed_ref[...] = total.reshape(units, C, D).astype(BF16)


def pack_kernel(src_ref, dst_ref):
    for h in range(dst_ref.shape[0]):
        dst_ref[h] = src_ref[:, h * D : (h + 1) * D]


def pack_extra_kernel(src_ref, beta_ref, decay_ref, dst_ref):
    beta = beta_ref[...].astype(F32)
    decay = decay_ref[...].astype(F32)
    zero = jnp.zeros((EXTRA - 2, C), F32)
    for h in range(dst_ref.shape[0]):
        one = slice(h, h + 1)
        dst_ref[h, :C] = src_ref[:, h * D : (h + 1) * D]
        dst_ref[h, C:] = jnp.concatenate([beta[one], decay[one], zero], axis=0).astype(BF16)


def unpack_kernel(src_ref, dst_ref):
    for h in range(src_ref.shape[0]):
        dst_ref[:, h * D : (h + 1) * D] = src_ref[h]


def blocks(units, *tail, flip=None, group=0):
    back = (0,) * (len(tail) - 1)
    if flip is None:
        return pl.BlockSpec((units,) + tail, lambda i: (i, group) + back)
    return pl.BlockSpec((units,) + tail, lambda i: (flip - 1 - i, group) + back)


SCALARS = [pl.BlockSpec(memory_space=pltpu.SMEM)] * 2


def params():
    return pltpu.CompilerParams(vmem_limit_bytes=VMEM_MIB * 1024 * 1024)


def cost(flops, moved):
    return pl.CostEstimate(flops=flops, bytes_accessed=moved, transcendentals=0)


def pack(array, extra=None, units=16):
    own, width = array.shape
    heads = width // D
    rows = own + (EXTRA if extra is not None else 0)
    return pl.pallas_call(
        pack_kernel if extra is None else pack_extra_kernel,
        grid=(heads // units,),
        in_specs=[pl.BlockSpec((own, units * D), lambda i: (0, i))]
        + ([] if extra is None else [pl.BlockSpec((units, own), lambda i: (i, 0))] * 2),
        out_specs=blocks(units, rows, D),
        out_shape=jax.ShapeDtypeStruct((heads, rows, D), BF16),
        compiler_params=params(),
        cost_estimate=cost(0, 4_000_000),
        name="pack",
    )(*([array] if extra is None else [array, *extra]))


def unpack(array, units=16):
    heads, own, _ = array.shape
    return pl.pallas_call(
        unpack_kernel,
        grid=(heads // units,),
        in_specs=[blocks(units, own, D)],
        out_specs=pl.BlockSpec((own, units * D), lambda i: (0, i)),
        out_shape=jax.ShapeDtypeStruct((own, heads * D), BF16),
        compiler_params=params(),
        cost_estimate=cost(0, 4_000_000),
        name="unpack",
    )(array)


def triples(chunks, count=3):
    return jax.ShapeDtypeStruct((chunks, count, C, 2 * D), BF16)


def run_keys(starts, base, kmsg, units=8):
    chunks = kmsg.shape[0]
    return pl.pallas_call(
        functools.partial(key_kernel, units),
        grid=(chunks // units,),
        in_specs=SCALARS + [blocks(units, C + EXTRA, D)],
        out_specs=[blocks(units, 9, C, 2 * D), blocks(units, D, C), blocks(units, 8, C)],
        out_shape=[
            triples(chunks, 9),
            jax.ShapeDtypeStruct((chunks, D, C), BF16),
            jax.ShapeDtypeStruct((chunks, 8, C), F32),
        ],
        compiler_params=params(),
        cost_estimate=cost(20_000_000_000, 20_000_000),
        name="key_maps",
    )(starts, base, kmsg)


def run_scan(starts, base, v, maps, units=8):
    chunks = v.shape[0]
    n = chunks // units
    return pl.pallas_call(
        functools.partial(scan_kernel, units, chunks),
        grid=(n,),
        in_specs=SCALARS
        + [blocks(units, 3, C, 2 * D), blocks(units, C, D)]
        + [blocks(units, 3, C, 2 * D, flip=n, group=1), blocks(units, C, D, flip=n)],
        out_specs=[blocks(units, 3, C, 2 * D), blocks(units, 3, C, 2 * D, flip=n)]
        + [pl.BlockSpec((3, D, D), lambda i: (0, 0, 0))],
        out_shape=[triples(chunks)] * 2 + [jax.ShapeDtypeStruct((3, D, D), F32)],
        scratch_shapes=[pltpu.VMEM((D, 2 * D), F32)] * 2,
        compiler_params=params(),
        cost_estimate=cost(20_000_000_000, 20_000_000),
        name="scan",
    )(starts, base, maps, v, maps, v)


def run_queries(q, kt, maps, rows, zf, zb, units=16):
    chunks = q.shape[0]
    return pl.pallas_call(
        functools.partial(query_kernel, units),
        grid=(chunks // units,),
        in_specs=[blocks(units, C, D), blocks(units, D, C)]
        + [blocks(units, 3, C, 2 * D, group=2), blocks(units, 8, C)]
        + [blocks(units, 3, C, 2 * D)] * 2,
        out_specs=blocks(units, 3, C, 2 * D),
        out_shape=triples(chunks),
        compiler_params=params(),
        cost_estimate=cost(20_000_000_000, 20_000_000),
        name="local_out",
    )(q, kt, maps, rows, zf, zb)


def run_final(starts, base, f, arrived, units=16):
    chunks = f.shape[0]
    whole = pl.BlockSpec((3, D, D), lambda i: (0, 0, 0))
    return pl.pallas_call(
        functools.partial(final_kernel, units, chunks * C),
        grid=(chunks // units,),
        in_specs=SCALARS + [blocks(units, 3, C, 2 * D)] + [whole] * 3,
        out_specs=blocks(units, C, D),
        out_shape=jax.ShapeDtypeStruct((chunks, C, D), BF16),
        scratch_shapes=[pltpu.VMEM((2 * D, 2 * D), BF16)],
        compiler_params=params(),
        cost_estimate=cost(2_000_000_000, 10_000_000),
        name="final",
    )(starts, base, f, *arrived)


def spread(array):
    return lax.all_to_all(array, GROUP, split_axis=0, concat_axis=0, tiled=True)


def on_device(queries, keys, values, beta, log_decay, seg_lengths):
    heads = queries.shape[1] // D
    groups = lax.axis_size("x")
    order = jnp.arange(seg_lengths.shape[0])
    starts = jnp.sum(jnp.where(order[None, :] < order[:, None], seg_lengths[None, :], 0), axis=1)
    starts = starts.astype(jnp.int32)
    base = (lax.axis_index("x") * heads * C).astype(jnp.int32).reshape(1)
    kmsg = spread(pack(keys, (beta.T, log_decay.T)))
    v = spread(pack(values))
    q = spread(pack(queries))
    maps, kt, rows = run_keys(starts, base, kmsg)
    zf, zb, total = run_scan(starts, base, v, maps)
    arrived = [
        lax.ppermute(total, "x", [(i, (i + d) % groups) for i in range(groups)]) for d in (1, 2, 3)
    ]
    f = run_queries(q, kt, maps, rows, zf, zb)
    return unpack(spread(run_final(starts, base, f, arrived)))


def solution(mesh):
    fine = Mesh(mesh.devices.reshape(4, 4, 4, 2), ("x", "y", "z", "core"))
    rows = P(("x", "y", "z", "core"), None)
    return jax.shard_map(
        on_device,
        mesh=fine,
        in_specs=(rows,) * 5 + (P(),),
        out_specs=rows,
        check_vma=False,
    )
```

```python
import functools

import jax
import jax.numpy as jnp
from jax import lax
from jax.experimental import pallas as pl
from jax.experimental.pallas import tpu as pltpu
from jax.sharding import Mesh, PartitionSpec as P

D = 128
C = 128
BASE = 16
EXTRA = 16
CUT = 128.0
VMEM_MIB = 50
F32 = jnp.float32
BF16 = jnp.bfloat16
GROUP = ("y", "z", "core")


def split(x):
    hi = x.astype(BF16)
    return hi, (x - hi.astype(F32)).astype(BF16)


def mm(a, b):
    return lax.dot_general(a, b, (((1,), (0,)), ((), ())), preferred_element_type=F32)


def lhs3(pair):
    return jnp.concatenate([pair[0], pair[1], pair[0]], axis=1)


def rhs3(pair):
    return jnp.concatenate([pair[0], pair[0], pair[1]], axis=0)


def dot3(a, b):
    return mm(lhs3(split(a)), rhs3(split(b)))


def beside(x):
    return jnp.concatenate(split(x), axis=1)


def below(x):
    return jnp.concatenate(split(x), axis=0)


def twice(b, axis):
    return jnp.concatenate([b, b], axis=axis)


def widen(ab):
    return jnp.concatenate([ab, ab[:, : ab.shape[1] // 2]], axis=1)


def halves(ab):
    return ab[:, : ab.shape[1] // 2], ab[:, ab.shape[1] // 2 :]


def deepen(hi, lo):
    return jnp.concatenate([hi, hi, lo], axis=0)


def iota(shape, dim):
    return lax.broadcasted_iota(jnp.int32, shape, dim)


def key_kernel(units, starts_ref, base_ref, kmsg_ref, maps_ref, kt_ref, rows_ref):
    step = pl.program_id(0)
    row, col = iota((C, C), 0), iota((C, C), 1)
    extra = kmsg_ref[:, C : C + EXTRA, :].astype(F32)
    beta = jnp.concatenate([extra[u, 0:1] for u in range(units)], axis=0)
    logd = jnp.concatenate([extra[u, 1:2] for u in range(units)], axis=0)
    level = mm(logd.astype(BF16), (row <= col).astype(BF16))
    begin = base_ref[0] + (step * units + iota((units, C), 0)) * C
    place = begin + iota((units, C), 1)
    cuts = jnp.zeros((units, C), F32)
    for n in range(starts_ref.shape[0]):
        at = starts_ref[n]
        cuts += jnp.where((begin < at) & (at <= place), 1.0, 0.0)
    level = level - CUT * cuts
    last = level[:, C - 1 : C]
    carried = jnp.exp(level)
    trail = jnp.exp(last - level)
    gate = jnp.exp(logd)
    inverse_gate = jnp.exp(-logd)
    eye = row == col
    keys = [kmsg_ref[u, :C, :] for u in range(units)]
    turned = [k.T for k in keys]
    gram = [mm(keys[u], turned[u]) for u in range(units)]
    norm = jnp.concatenate(
        [jnp.sum(jnp.where(eye, g, 0.0), axis=0, keepdims=True) for g in gram], axis=0
    )
    scale = 1.0 / jnp.sqrt(norm + 1e-6)
    columns = jnp.concatenate(
        [level, beta * scale, beta, carried * scale, trail * scale], axis=0
    ).T

    def column(which, u):
        return columns[:, which * units + u : which * units + u + 1]

    same = (row // BASE) == (col // BASE)
    systems, compact = [], []
    for u in range(units):
        decay = jnp.exp(-jnp.abs(column(0, u) - level[u : u + 1]))
        weighted = decay * scale[u : u + 1]
        maps_ref[u, 8] = beside(weighted)
        system = jnp.where(row > col, gram[u] * weighted * column(1, u), 0.0)
        systems.append(system)
        inside = jnp.where(same, system, 0.0)
        compact.append(sum(inside[i * BASE : (i + 1) * BASE] for i in range(C // BASE)))
    lane = iota((BASE, C), 1)
    small_row = iota((BASE, C), 0)
    solved = [jnp.where(small_row == lane % BASE, 1.0, 0.0) for u in range(units)]
    first = (lane // BASE) * BASE
    for j in range(BASE - 1):
        top = (j // 8) * 8
        for u in range(units):
            factor = jnp.take_along_axis(compact[u][top:], first[top:] + j, axis=1)
            low = solved[u][top:] - factor * solved[u][j : j + 1]
            solved[u] = jnp.concatenate([solved[u][:top], low], axis=0) if top else low
    full = [
        jnp.where(same, jnp.concatenate([solved[u]] * (C // BASE), axis=0), 0.0)
        for u in range(units)
    ]
    half_row, half_col = iota((C // 2, C), 0), iota((C // 2, C), 1)
    size = BASE
    while size < C:
        pieces = range(C // (2 * size))

        def lower_rows(t):
            return jnp.concatenate([t[(2 * i + 1) * size : (2 * i + 2) * size] for i in pieces], axis=0)

        inside = (half_col // size) == 2 * (half_row // size)
        zero = jnp.zeros((size, C), F32)
        part = [
            dot3(jnp.where(inside, lower_rows(systems[u]), 0.0), full[u]) for u in range(units)
        ]
        for u in range(units):
            rows = [part[u][i * size : (i + 1) * size] for i in pieces]
            spread = jnp.concatenate([block for r in rows for block in (zero, r)], axis=0)
            part[u] = dot3(lower_rows(full[u]), spread)
        for u in range(units):
            t = full[u]
            blocks_of = []
            for i in pieces:
                blocks_of.append(t[2 * i * size : (2 * i + 1) * size])
                blocks_of.append(
                    t[(2 * i + 1) * size : (2 * i + 2) * size] - part[u][i * size : (i + 1) * size]
                )
            full[u] = jnp.concatenate(blocks_of, axis=0)
        size *= 2
    both = [None] * units
    for u in range(units):
        one = slice(u, u + 1)
        kt_ref[u] = turned[u]
        y = full[u] * beta[one]
        yt = full[u].T * column(2, u)
        maps_ref[u, 2] = beside(y)
        maps_ref[u, 5] = beside(yt * inverse_gate[one])
        right = jnp.concatenate([y * column(4, u), yt * column(3, u)], axis=1)
        both[u] = mm(twice(turned[u], 1), below(right))
    rests = [None] * units
    for u in range(units):
        one = slice(u, u + 1)
        xt, wt = both[u][:, :C], both[u][:, C:]
        rests[u] = mm(beside(xt * (carried[one] * scale[one])), twice(keys[u], 0))
        maps_ref[u, 1] = beside(xt)
        maps_ref[u, 4] = beside(wt * inverse_gate[one])
        maps_ref[u, 6] = beside(wt.T)
        maps_ref[u, 7] = beside(xt.T)
        rows_ref[u] = jnp.concatenate(
            [carried[one], trail[one], gate[one], jnp.zeros((5, C), F32)], axis=0
        )
    for u in range(units):
        at = jnp.where(eye, carried[u : u + 1, C - 1 : C], 0.0) - rests[u]
        maps_ref[u, 0] = beside(at)
        maps_ref[u, 3] = beside(at.T)


def is_start(starts_ref, at):
    found = starts_ref[0] == at
    for n in range(1, starts_ref.shape[0]):
        found = found | (starts_ref[n] == at)
    return found


def keep(cut):
    return jnp.where(cut, 0.0, 1.0)


def scan_kernel(
    units, chunks, starts_ref, base_ref, ff_ref, vf_ref, bb_ref, vb_ref,
    zf_ref, zb_ref, total_ref, forward, backward,
):
    step = pl.program_id(0)

    @pl.when(step == 0)
    def _():
        eye = jnp.where(iota((D, D), 0) == iota((D, D), 1), 1.0, 0.0)
        start = jnp.concatenate([jnp.zeros((D, D), F32), eye], axis=1)
        forward[...] = start
        backward[...] = start

    zero = jnp.zeros((D, D), F32)

    def prepare(maps_ref, v_ref, z_ref, u):
        both = mm(maps_ref[u, 1:3].reshape(2 * C, 2 * D), twice(v_ref[u], 0))
        z_ref[u, 2] = beside(both[C:])
        return both[:C]

    def keep_state(z_ref, u, z):
        pair = split(z)
        z_ref[u, 0], z_ref[u, 1] = pair
        return pair

    def beyond(inject):
        return jnp.concatenate([inject, zero], axis=1)

    def keeps(u):
        n = step * units + u
        cut_f = is_start(starts_ref, base_ref[0] + n * C) & (n > 0)
        cut_b = is_start(starts_ref, base_ref[0] + (chunks - n) * C) & (n > 0)
        return keep(cut_f), keep(cut_b)

    inject_f = [prepare(ff_ref, vf_ref, zf_ref, u) for u in range(units)]
    inject_b = [prepare(bb_ref, vb_ref, zb_ref, u) for u in range(units)]
    last = units - 1
    zf, zb = forward[...], backward[...]
    for u in range(units):
        r = last - u
        kept_f, kept_b = keeps(u)
        pair_f = keep_state(zf_ref, u, zf * kept_f)
        pair_b = keep_state(zb_ref, r, zb * kept_b)
        zf = mm(widen(ff_ref[u, 0]), deepen(*pair_f)) + beyond(inject_f[u])
        zb = mm(widen(bb_ref[r, 0]), deepen(*pair_b)) + beyond(inject_b[r])
    forward[...] = zf
    backward[...] = zb
    total_ref[0] = zf[:, D:]
    total_ref[1] = zf[:, :D]
    total_ref[2] = zb[:, :D]


def query_kernel(units, q_ref, kt_ref, maps_ref, rows_ref, zf_ref, zb_ref, f_ref):
    row, col = iota((C, C), 0), iota((C, C), 1)

    def pairs(one, two):
        one_hi, one_lo = halves(one)
        two_hi, two_lo = halves(two)
        return deepen(
            jnp.concatenate([one_hi, two_hi], axis=1), jnp.concatenate([one_lo, two_lo], axis=1)
        )

    every = range(units)
    columns = [rows_ref[u].T for u in every]
    scores = [mm(q_ref[u], kt_ref[u]) for u in every]
    first, second = [None] * units, [None] * units
    for u in every:
        se_hi, se_lo = halves(maps_ref[u, 2])
        score = scores[u] * (se_hi.astype(F32) + se_lo.astype(F32))
        lower = beside(jnp.where(col <= row, score, 0.0))
        upper = beside(jnp.where(col > row, score, 0.0))
        first[u] = mm(widen(lower), pairs(zf_ref[u, 2], maps_ref[u, 0]))
        second[u] = mm(widen(upper), pairs(zb_ref[u, 2], maps_ref[u, 1]))
    third, fourth = [None] * units, [None] * units
    for u in every:
        carried, trail, gate = (columns[u][:, i : i + 1] for i in range(3))
        q = q_ref[u].astype(F32)
        effect_f = carried * q - first[u][:, D:]
        effect_b = gate * (trail * q - second[u][:, D:])
        third[u] = mm(widen(beside(effect_f)), deepen(zf_ref[u, 0], zf_ref[u, 1]))
        fourth[u] = mm(widen(beside(effect_b)), deepen(zb_ref[u, 0], zb_ref[u, 1]))
    for u in every:
        gate = columns[u][:, 2:3]
        total = first[u][:, :D] + gate * second[u][:, :D] + third[u][:, :D] + fourth[u][:, :D]
        f_ref[u, 0] = beside(total)
        hi, lo = split(jnp.concatenate([third[u][:, D:], fourth[u][:, D:]], axis=1))
        f_ref[u, 1] = hi
        f_ref[u, 2] = lo


def final_kernel(units, span, starts_ref, base_ref, f_ref, one_ref, two_ref, three_ref, mixed_ref, state):
    step = pl.program_id(0)

    @pl.when(step == 0)
    def _():
        mine = base_ref[0] // span
        arrived = {1: one_ref, 2: two_ref, 3: three_ref}
        turned = {d: arrived[d][0].T for d in arrived}
        sf = jnp.zeros((D, D), F32)
        sb = jnp.zeros((D, D), F32)
        for d in (1, 2, 3):
            e = 4 - d
            cut = is_start(starts_ref, (mine - e) * span)
            moved = dot3(arrived[e][0], sf * keep(cut)) + arrived[e][1]
            sf = jnp.where(e <= mine, moved, sf)
            cut = is_start(starts_ref, (mine - d + 5) * span)
            moved = dot3(turned[d], sb * keep(cut)) + arrived[d][2]
            sb = jnp.where(d > mine, moved, sb)
        sf = sf * keep(is_start(starts_ref, mine * span))
        sb = sb * keep(is_start(starts_ref, (mine + 1) * span))
        state[...] = beside(jnp.concatenate([sf, sb], axis=0))

    def rows_of(which):
        return f_ref[:, which].reshape(units * C, 2 * D)

    wide = mm(rows_of(1), state[...])
    more = mm(rows_of(2), state[:, :D])
    hi, lo = halves(rows_of(0))
    total = (hi.astype(F32) + lo.astype(F32)) + (wide[:, :D] + wide[:, D:] + more)
    mixed_ref[...] = total.reshape(units, C, D).astype(BF16)


def pack_kernel(src_ref, dst_ref):
    for h in range(dst_ref.shape[0]):
        dst_ref[h] = src_ref[:, h * D : (h + 1) * D]


def pack_extra_kernel(src_ref, beta_ref, decay_ref, dst_ref):
    beta = beta_ref[...].astype(F32)
    decay = decay_ref[...].astype(F32)
    zero = jnp.zeros((EXTRA - 2, C), F32)
    for h in range(dst_ref.shape[0]):
        one = slice(h, h + 1)
        dst_ref[h, :C] = src_ref[:, h * D : (h + 1) * D]
        dst_ref[h, C:] = jnp.concatenate([beta[one], decay[one], zero], axis=0).astype(BF16)


def unpack_kernel(src_ref, dst_ref):
    for h in range(src_ref.shape[0]):
        dst_ref[:, h * D : (h + 1) * D] = src_ref[h]


def blocks(units, *tail, flip=None, group=0):
    back = (0,) * (len(tail) - 1)
    if flip is None:
        return pl.BlockSpec((units,) + tail, lambda i: (i, group) + back)
    return pl.BlockSpec((units,) + tail, lambda i: (flip - 1 - i, group) + back)


SCALARS = [pl.BlockSpec(memory_space=pltpu.SMEM)] * 2


def params(mib=VMEM_MIB):
    return pltpu.CompilerParams(vmem_limit_bytes=mib * 1024 * 1024)


def cost(flops, moved):
    return pl.CostEstimate(flops=flops, bytes_accessed=moved, transcendentals=0)


def pack(array, extra=None, units=16):
    own, width = array.shape
    heads = width // D
    rows = own + (EXTRA if extra is not None else 0)
    return pl.pallas_call(
        pack_kernel if extra is None else pack_extra_kernel,
        grid=(heads // units,),
        in_specs=[pl.BlockSpec((own, units * D), lambda i: (0, i))]
        + ([] if extra is None else [pl.BlockSpec((units, own), lambda i: (i, 0))] * 2),
        out_specs=blocks(units, rows, D),
        out_shape=jax.ShapeDtypeStruct((heads, rows, D), BF16),
        compiler_params=params(60),
        cost_estimate=cost(0, 4_000_000),
        name="pack",
    )(*([array] if extra is None else [array, *extra]))


def unpack(array, units=16):
    heads, own, _ = array.shape
    return pl.pallas_call(
        unpack_kernel,
        grid=(heads // units,),
        in_specs=[blocks(units, own, D)],
        out_specs=pl.BlockSpec((own, units * D), lambda i: (0, i)),
        out_shape=jax.ShapeDtypeStruct((own, heads * D), BF16),
        compiler_params=params(60),
        cost_estimate=cost(0, 4_000_000),
        name="unpack",
    )(array)


def triples(chunks, count=3):
    return jax.ShapeDtypeStruct((chunks, count, C, 2 * D), BF16)


def run_keys(starts, base, kmsg, units=8):
    chunks = kmsg.shape[0]
    return pl.pallas_call(
        functools.partial(key_kernel, units),
        grid=(chunks // units,),
        in_specs=SCALARS + [blocks(units, C + EXTRA, D)],
        out_specs=[blocks(units, 9, C, 2 * D), blocks(units, D, C), blocks(units, 8, C)],
        out_shape=[
            triples(chunks, 9),
            jax.ShapeDtypeStruct((chunks, D, C), BF16),
            jax.ShapeDtypeStruct((chunks, 8, C), F32),
        ],
        compiler_params=params(),
        cost_estimate=cost(20_000_000_000, 20_000_000),
        name="key_maps",
    )(starts, base, kmsg)


def run_scan(starts, base, v, maps, units=8):
    chunks = v.shape[0]
    n = chunks // units
    return pl.pallas_call(
        functools.partial(scan_kernel, units, chunks),
        grid=(n,),
        in_specs=SCALARS
        + [blocks(units, 3, C, 2 * D), blocks(units, C, D)]
        + [blocks(units, 3, C, 2 * D, flip=n, group=1), blocks(units, C, D, flip=n)],
        out_specs=[blocks(units, 3, C, 2 * D), blocks(units, 3, C, 2 * D, flip=n)]
        + [pl.BlockSpec((3, D, D), lambda i: (0, 0, 0))],
        out_shape=[triples(chunks)] * 2 + [jax.ShapeDtypeStruct((3, D, D), F32)],
        scratch_shapes=[pltpu.VMEM((D, 2 * D), F32)] * 2,
        compiler_params=params(),
        cost_estimate=cost(20_000_000_000, 20_000_000),
        name="scan",
    )(starts, base, maps, v, maps, v)


def run_queries(q, kt, maps, rows, zf, zb, units=16):
    chunks = q.shape[0]
    return pl.pallas_call(
        functools.partial(query_kernel, units),
        grid=(chunks // units,),
        in_specs=[blocks(units, C, D), blocks(units, D, C)]
        + [blocks(units, 3, C, 2 * D, group=2), blocks(units, 8, C)]
        + [blocks(units, 3, C, 2 * D)] * 2,
        out_specs=blocks(units, 3, C, 2 * D),
        out_shape=triples(chunks),
        compiler_params=params(36),
        cost_estimate=cost(20_000_000_000, 20_000_000),
        name="local_out",
    )(q, kt, maps, rows, zf, zb)


def run_final(starts, base, f, arrived, units=16):
    chunks = f.shape[0]
    whole = pl.BlockSpec((3, D, D), lambda i: (0, 0, 0))
    return pl.pallas_call(
        functools.partial(final_kernel, units, chunks * C),
        grid=(chunks // units,),
        in_specs=SCALARS + [blocks(units, 3, C, 2 * D)] + [whole] * 3,
        out_specs=blocks(units, C, D),
        out_shape=jax.ShapeDtypeStruct((chunks, C, D), BF16),
        scratch_shapes=[pltpu.VMEM((2 * D, 2 * D), BF16)],
        compiler_params=params(36),
        cost_estimate=cost(2_000_000_000, 10_000_000),
        name="final",
    )(starts, base, f, *arrived)


def spread(array):
    return lax.all_to_all(array, GROUP, split_axis=0, concat_axis=0, tiled=True)


def on_device(queries, keys, values, beta, log_decay, seg_lengths):
    heads = queries.shape[1] // D
    groups = lax.axis_size("x")
    order = jnp.arange(seg_lengths.shape[0])
    starts = jnp.sum(jnp.where(order[None, :] < order[:, None], seg_lengths[None, :], 0), axis=1)
    starts = starts.astype(jnp.int32)
    base = (lax.axis_index("x") * heads * C).astype(jnp.int32).reshape(1)
    kmsg = spread(pack(keys, (beta.T, log_decay.T)))
    v = spread(pack(values))
    q = spread(pack(queries))
    maps, kt, rows = run_keys(starts, base, kmsg)
    zf, zb, total = run_scan(starts, base, v, maps)
    arrived = [
        lax.ppermute(total, "x", [(i, (i + d) % groups) for i in range(groups)]) for d in (1, 2, 3)
    ]
    f = run_queries(q, kt, maps, rows, zf, zb)
    return unpack(spread(run_final(starts, base, f, arrived)))


def solution(mesh):
    fine = Mesh(mesh.devices.reshape(4, 4, 4, 2), ("x", "y", "z", "core"))
    rows = P(("x", "y", "z", "core"), None)
    return jax.shard_map(
        on_device,
        mesh=fine,
        in_specs=(rows,) * 5 + (P(),),
        out_specs=rows,
        check_vma=False,
    )
```

```python
import functools

import jax
import jax.numpy as jnp
from jax import lax
from jax.experimental import pallas as pl
from jax.experimental.pallas import tpu as pltpu
from jax.sharding import Mesh, PartitionSpec as P

D = 128
C = 128
BASE = 16
EXTRA = 16
CUT = 128.0
VMEM_MIB = 50
F32 = jnp.float32
BF16 = jnp.bfloat16
GROUP = ("y", "z", "core")


def split(x):
    hi = x.astype(BF16)
    return hi, (x - hi.astype(F32)).astype(BF16)


def mm(a, b):
    return lax.dot_general(a, b, (((1,), (0,)), ((), ())), preferred_element_type=F32)


def lhs3(pair):
    return jnp.concatenate([pair[0], pair[1], pair[0]], axis=1)


def rhs3(pair):
    return jnp.concatenate([pair[0], pair[0], pair[1]], axis=0)


def dot3(a, b):
    return mm(lhs3(split(a)), rhs3(split(b)))


def beside(x):
    return jnp.concatenate(split(x), axis=1)


def below(x):
    return jnp.concatenate(split(x), axis=0)


def twice(b, axis):
    return jnp.concatenate([b, b], axis=axis)


def widen(ab):
    return jnp.concatenate([ab, ab[:, : ab.shape[1] // 2]], axis=1)


def halves(ab):
    return ab[:, : ab.shape[1] // 2], ab[:, ab.shape[1] // 2 :]


def deepen(hi, lo):
    return jnp.concatenate([hi, hi, lo], axis=0)


def iota(shape, dim):
    return lax.broadcasted_iota(jnp.int32, shape, dim)


def key_kernel(units, starts_ref, base_ref, kmsg_ref, maps_ref):
    step = pl.program_id(0)
    row, col = iota((C, C), 0), iota((C, C), 1)
    extra = kmsg_ref[:, C : C + EXTRA, :].astype(F32)
    beta = jnp.concatenate([extra[u, 0:1] for u in range(units)], axis=0)
    logd = jnp.concatenate([extra[u, 1:2] for u in range(units)], axis=0)
    level = mm(logd.astype(BF16), (row <= col).astype(BF16))
    begin = base_ref[0] + (step * units + iota((units, C), 0)) * C
    place = begin + iota((units, C), 1)
    cuts = jnp.zeros((units, C), F32)
    for n in range(starts_ref.shape[0]):
        at = starts_ref[n]
        cuts += jnp.where((begin < at) & (at <= place), 1.0, 0.0)
    level = level - CUT * cuts
    last = level[:, C - 1 : C]
    carried = jnp.exp(level)
    trail = jnp.exp(last - level)
    gate = jnp.exp(logd)
    inverse_gate = jnp.exp(-logd)
    eye = row == col
    keys = [kmsg_ref[u, :C, :] for u in range(units)]
    turned = [k.T for k in keys]
    gram = [mm(keys[u], turned[u]) for u in range(units)]
    norm = jnp.concatenate(
        [jnp.sum(jnp.where(eye, g, 0.0), axis=0, keepdims=True) for g in gram], axis=0
    )
    scale = 1.0 / jnp.sqrt(norm + 1e-6)
    columns = jnp.concatenate(
        [level, beta * scale, beta, carried * scale, trail * scale], axis=0
    ).T

    def column(which, u):
        return columns[:, which * units + u : which * units + u + 1]

    same = (row // BASE) == (col // BASE)
    systems, compact = [], []
    for u in range(units):
        decay = jnp.exp(-jnp.abs(column(0, u) - level[u : u + 1]))
        weighted = decay * scale[u : u + 1]
        maps_ref[u, 8] = beside(weighted)
        system = jnp.where(row > col, gram[u] * weighted * column(1, u), 0.0)
        systems.append(system)
        inside = jnp.where(same, system, 0.0)
        compact.append(sum(inside[i * BASE : (i + 1) * BASE] for i in range(C // BASE)))
    lane = iota((BASE, C), 1)
    small_row = iota((BASE, C), 0)
    solved = [jnp.where(small_row == lane % BASE, 1.0, 0.0) for u in range(units)]
    first = (lane // BASE) * BASE
    for j in range(BASE - 1):
        top = (j // 8) * 8
        for u in range(units):
            factor = jnp.take_along_axis(compact[u][top:], first[top:] + j, axis=1)
            low = solved[u][top:] - factor * solved[u][j : j + 1]
            solved[u] = jnp.concatenate([solved[u][:top], low], axis=0) if top else low
    full = [
        jnp.where(same, jnp.concatenate([solved[u]] * (C // BASE), axis=0), 0.0)
        for u in range(units)
    ]
    half_row, half_col = iota((C // 2, C), 0), iota((C // 2, C), 1)
    size = BASE
    while size < C:
        pieces = range(C // (2 * size))

        def lower_rows(t):
            return jnp.concatenate([t[(2 * i + 1) * size : (2 * i + 2) * size] for i in pieces], axis=0)

        inside = (half_col // size) == 2 * (half_row // size)
        zero = jnp.zeros((size, C), F32)
        part = [
            dot3(jnp.where(inside, lower_rows(systems[u]), 0.0), full[u]) for u in range(units)
        ]
        for u in range(units):
            rows = [part[u][i * size : (i + 1) * size] for i in pieces]
            spread = jnp.concatenate([block for r in rows for block in (zero, r)], axis=0)
            part[u] = dot3(lower_rows(full[u]), spread)
        for u in range(units):
            t = full[u]
            blocks_of = []
            for i in pieces:
                blocks_of.append(t[2 * i * size : (2 * i + 1) * size])
                blocks_of.append(
                    t[(2 * i + 1) * size : (2 * i + 2) * size] - part[u][i * size : (i + 1) * size]
                )
            full[u] = jnp.concatenate(blocks_of, axis=0)
        size *= 2
    both = [None] * units
    for u in range(units):
        one = slice(u, u + 1)
        y = full[u] * beta[one]
        yt = full[u].T * column(2, u)
        maps_ref[u, 2] = beside(y)
        maps_ref[u, 5] = beside(yt * inverse_gate[one])
        right = jnp.concatenate([y * column(4, u), yt * column(3, u)], axis=1)
        both[u] = mm(twice(turned[u], 1), below(right))
    rests = [None] * units
    for u in range(units):
        one = slice(u, u + 1)
        xt, wt = both[u][:, :C], both[u][:, C:]
        rests[u] = mm(beside(xt * (carried[one] * scale[one])), twice(keys[u], 0))
        maps_ref[u, 1] = beside(xt)
        maps_ref[u, 4] = beside(wt * inverse_gate[one])
        maps_ref[u, 6] = beside(wt.T)
        maps_ref[u, 7] = beside(xt.T)
        rows = jnp.concatenate([carried[one], trail[one], gate[one], jnp.zeros((5, C), F32)], axis=0)
        hi = rows.astype(BF16).astype(F32)
        rows = jnp.concatenate([hi, rows - hi, jnp.zeros((C - 16, C), F32)], axis=0).astype(BF16)
        maps_ref[u, 9] = jnp.concatenate([turned[u], rows], axis=1)
    for u in range(units):
        at = jnp.where(eye, carried[u : u + 1, C - 1 : C], 0.0) - rests[u]
        maps_ref[u, 0] = beside(at)
        maps_ref[u, 3] = beside(at.T)


def is_start(starts_ref, at):
    found = starts_ref[0] == at
    for n in range(1, starts_ref.shape[0]):
        found = found | (starts_ref[n] == at)
    return found


def keep(cut):
    return jnp.where(cut, 0.0, 1.0)


def scan_kernel(
    units, chunks, starts_ref, base_ref, ff_ref, vf_ref, bb_ref, vb_ref,
    zf_ref, zb_ref, total_ref, forward, backward,
):
    step = pl.program_id(0)

    @pl.when(step == 0)
    def _():
        eye = jnp.where(iota((D, D), 0) == iota((D, D), 1), 1.0, 0.0)
        start = jnp.concatenate([jnp.zeros((D, D), F32), eye], axis=1)
        forward[...] = start
        backward[...] = start

    zero = jnp.zeros((D, D), F32)

    def prepare(maps_ref, v_ref, z_ref, u):
        both = mm(maps_ref[u, 1:3].reshape(2 * C, 2 * D), twice(v_ref[u], 0))
        z_ref[u, 2] = beside(both[C:])
        return both[:C]

    def keep_state(z_ref, u, z):
        pair = split(z)
        z_ref[u, 0], z_ref[u, 1] = pair
        return pair

    def beyond(inject):
        return jnp.concatenate([inject, zero], axis=1)

    def keeps(u):
        n = step * units + u
        cut_f = is_start(starts_ref, base_ref[0] + n * C) & (n > 0)
        cut_b = is_start(starts_ref, base_ref[0] + (chunks - n) * C) & (n > 0)
        return keep(cut_f), keep(cut_b)

    inject_f, inject_b = {}, {}

    def ready(u):
        if u < units:
            inject_f[u] = prepare(ff_ref, vf_ref, zf_ref, u)
            inject_b[units - 1 - u] = prepare(bb_ref, vb_ref, zb_ref, units - 1 - u)

    ready(0)
    last = units - 1
    zf, zb = forward[...], backward[...]
    for u in range(units):
        r = last - u
        kept_f, kept_b = keeps(u)
        pair_f = keep_state(zf_ref, u, zf * kept_f)
        pair_b = keep_state(zb_ref, r, zb * kept_b)
        zf = mm(widen(ff_ref[u, 0]), deepen(*pair_f))
        zb = mm(widen(bb_ref[r, 0]), deepen(*pair_b))
        ready(u + 1)
        zf = zf + beyond(inject_f[u])
        zb = zb + beyond(inject_b[r])
    forward[...] = zf
    backward[...] = zb
    total_ref[0] = zf[:, D:]
    total_ref[1] = zf[:, :D]
    total_ref[2] = zb[:, :D]


def query_kernel(units, q_ref, maps_ref, more_ref, zf_ref, zb_ref, f_ref):
    row, col = iota((C, C), 0), iota((C, C), 1)

    def pairs(one, two):
        one_hi, one_lo = halves(one)
        two_hi, two_lo = halves(two)
        return deepen(
            jnp.concatenate([one_hi, two_hi], axis=1), jnp.concatenate([one_lo, two_lo], axis=1)
        )

    every = range(units)
    rows = [more_ref[u, 0, :16, C:].astype(F32) for u in every]
    columns = [(rows[u][:8] + rows[u][8:]).T for u in every]
    scores = [mm(q_ref[u], more_ref[u, 0, :, :C]) for u in every]
    first, second = [None] * units, [None] * units
    for u in every:
        se_hi, se_lo = halves(maps_ref[u, 2])
        score = scores[u] * (se_hi.astype(F32) + se_lo.astype(F32))
        lower = beside(jnp.where(col <= row, score, 0.0))
        upper = beside(jnp.where(col > row, score, 0.0))
        first[u] = mm(widen(lower), pairs(zf_ref[u, 2], maps_ref[u, 0]))
        second[u] = mm(widen(upper), pairs(zb_ref[u, 2], maps_ref[u, 1]))
    third, fourth = [None] * units, [None] * units
    for u in every:
        carried, trail, gate = (columns[u][:, i : i + 1] for i in range(3))
        q = q_ref[u].astype(F32)
        effect_f = carried * q - first[u][:, D:]
        effect_b = gate * (trail * q - second[u][:, D:])
        third[u] = mm(widen(beside(effect_f)), deepen(zf_ref[u, 0], zf_ref[u, 1]))
        fourth[u] = mm(widen(beside(effect_b)), deepen(zb_ref[u, 0], zb_ref[u, 1]))
    for u in every:
        gate = columns[u][:, 2:3]
        total = first[u][:, :D] + gate * second[u][:, :D] + third[u][:, :D] + fourth[u][:, :D]
        f_ref[u, 0] = beside(total)
        hi, lo = split(jnp.concatenate([third[u][:, D:], fourth[u][:, D:]], axis=1))
        f_ref[u, 1] = hi
        f_ref[u, 2] = lo


def final_kernel(units, span, starts_ref, base_ref, f_ref, one_ref, two_ref, three_ref, mixed_ref, state):
    step = pl.program_id(0)

    @pl.when(step == 0)
    def _():
        mine = base_ref[0] // span
        arrived = {1: one_ref, 2: two_ref, 3: three_ref}
        turned = {d: arrived[d][0].T for d in arrived}
        sf = jnp.zeros((D, D), F32)
        sb = jnp.zeros((D, D), F32)
        for d in (1, 2, 3):
            e = 4 - d
            cut = is_start(starts_ref, (mine - e) * span)
            moved = dot3(arrived[e][0], sf * keep(cut)) + arrived[e][1]
            sf = jnp.where(e <= mine, moved, sf)
            cut = is_start(starts_ref, (mine - d + 5) * span)
            moved = dot3(turned[d], sb * keep(cut)) + arrived[d][2]
            sb = jnp.where(d > mine, moved, sb)
        sf = sf * keep(is_start(starts_ref, mine * span))
        sb = sb * keep(is_start(starts_ref, (mine + 1) * span))
        state[...] = beside(jnp.concatenate([sf, sb], axis=0))

    def rows_of(which):
        return f_ref[:, which].reshape(units * C, 2 * D)

    wide = mm(rows_of(1), state[...])
    more = mm(rows_of(2), state[:, :D])
    hi, lo = halves(rows_of(0))
    total = (hi.astype(F32) + lo.astype(F32)) + (wide[:, :D] + wide[:, D:] + more)
    mixed_ref[...] = total.reshape(units, C, D).astype(BF16)


def pack_kernel(src_ref, dst_ref):
    for h in range(dst_ref.shape[0]):
        dst_ref[h] = src_ref[:, h * D : (h + 1) * D]


def pack_extra_kernel(src_ref, beta_ref, decay_ref, dst_ref):
    beta = beta_ref[...].astype(F32)
    decay = decay_ref[...].astype(F32)
    zero = jnp.zeros((EXTRA - 2, C), F32)
    for h in range(dst_ref.shape[0]):
        one = slice(h, h + 1)
        dst_ref[h, :C] = src_ref[:, h * D : (h + 1) * D]
        dst_ref[h, C:] = jnp.concatenate([beta[one], decay[one], zero], axis=0).astype(BF16)


def unpack_kernel(src_ref, dst_ref):
    for h in range(src_ref.shape[0]):
        dst_ref[:, h * D : (h + 1) * D] = src_ref[h]


def blocks(units, *tail, flip=None, group=0):
    back = (0,) * (len(tail) - 1)
    if flip is None:
        return pl.BlockSpec((units,) + tail, lambda i: (i, group) + back)
    return pl.BlockSpec((units,) + tail, lambda i: (flip - 1 - i, group) + back)


SCALARS = [pl.BlockSpec(memory_space=pltpu.SMEM)] * 2


def params(mib=VMEM_MIB):
    return pltpu.CompilerParams(vmem_limit_bytes=mib * 1024 * 1024)


def cost(flops, moved):
    return pl.CostEstimate(flops=flops, bytes_accessed=moved, transcendentals=0)


def pack(array, extra=None, units=16):
    own, width = array.shape
    heads = width // D
    rows = own + (EXTRA if extra is not None else 0)
    return pl.pallas_call(
        pack_kernel if extra is None else pack_extra_kernel,
        grid=(heads // units,),
        in_specs=[pl.BlockSpec((own, units * D), lambda i: (0, i))]
        + ([] if extra is None else [pl.BlockSpec((units, own), lambda i: (i, 0))] * 2),
        out_specs=blocks(units, rows, D),
        out_shape=jax.ShapeDtypeStruct((heads, rows, D), BF16),
        compiler_params=params(60),
        cost_estimate=cost(0, 4_000_000),
        name="pack",
    )(*([array] if extra is None else [array, *extra]))


def unpack(array, units=16):
    heads, own, _ = array.shape
    return pl.pallas_call(
        unpack_kernel,
        grid=(heads // units,),
        in_specs=[blocks(units, own, D)],
        out_specs=pl.BlockSpec((own, units * D), lambda i: (0, i)),
        out_shape=jax.ShapeDtypeStruct((own, heads * D), BF16),
        compiler_params=params(36),
        cost_estimate=cost(0, 4_000_000),
        name="unpack",
    )(array)


def triples(chunks, count=3):
    return jax.ShapeDtypeStruct((chunks, count, C, 2 * D), BF16)


def run_keys(starts, base, kmsg, units=8):
    chunks = kmsg.shape[0]
    return pl.pallas_call(
        functools.partial(key_kernel, units),
        grid=(chunks // units,),
        in_specs=SCALARS + [blocks(units, C + EXTRA, D)],
        out_specs=blocks(units, 10, C, 2 * D),
        out_shape=triples(chunks, 10),
        compiler_params=params(),
        cost_estimate=cost(20_000_000_000, 20_000_000),
        name="key_maps",
    )(starts, base, kmsg)


def run_scan(starts, base, v, maps, units=8):
    chunks = v.shape[0]
    n = chunks // units
    return pl.pallas_call(
        functools.partial(scan_kernel, units, chunks),
        grid=(n,),
        in_specs=SCALARS
        + [blocks(units, 3, C, 2 * D), blocks(units, C, D)]
        + [blocks(units, 3, C, 2 * D, flip=n, group=1), blocks(units, C, D, flip=n)],
        out_specs=[blocks(units, 3, C, 2 * D), blocks(units, 3, C, 2 * D, flip=n)]
        + [pl.BlockSpec((3, D, D), lambda i: (0, 0, 0))],
        out_shape=[triples(chunks)] * 2 + [jax.ShapeDtypeStruct((3, D, D), F32)],
        scratch_shapes=[pltpu.VMEM((D, 2 * D), F32)] * 2,
        compiler_params=params(),
        cost_estimate=cost(20_000_000_000, 20_000_000),
        name="scan",
    )(starts, base, maps, v, maps, v)


def run_queries(q, maps, zf, zb, units=16):
    chunks = q.shape[0]
    return pl.pallas_call(
        functools.partial(query_kernel, units),
        grid=(chunks // units,),
        in_specs=[blocks(units, C, D)]
        + [blocks(units, 3, C, 2 * D, group=2), blocks(units, 1, C, 2 * D, group=9)]
        + [blocks(units, 3, C, 2 * D)] * 2,
        out_specs=blocks(units, 3, C, 2 * D),
        out_shape=triples(chunks),
        compiler_params=params(36),
        cost_estimate=cost(20_000_000_000, 20_000_000),
        name="local_out",
    )(q, maps, maps, zf, zb)


def run_final(starts, base, f, arrived, units=16):
    chunks = f.shape[0]
    whole = pl.BlockSpec((3, D, D), lambda i: (0, 0, 0))
    return pl.pallas_call(
        functools.partial(final_kernel, units, chunks * C),
        grid=(chunks // units,),
        in_specs=SCALARS + [blocks(units, 3, C, 2 * D)] + [whole] * 3,
        out_specs=blocks(units, C, D),
        out_shape=jax.ShapeDtypeStruct((chunks, C, D), BF16),
        scratch_shapes=[pltpu.VMEM((2 * D, 2 * D), BF16)],
        compiler_params=params(36),
        cost_estimate=cost(2_000_000_000, 10_000_000),
        name="final",
    )(starts, base, f, *arrived)


def spread(array):
    return lax.all_to_all(array, GROUP, split_axis=0, concat_axis=0, tiled=True)


def on_device(queries, keys, values, beta, log_decay, seg_lengths):
    heads = queries.shape[1] // D
    groups = lax.axis_size("x")
    order = jnp.arange(seg_lengths.shape[0])
    starts = jnp.sum(jnp.where(order[None, :] < order[:, None], seg_lengths[None, :], 0), axis=1)
    starts = starts.astype(jnp.int32)
    base = (lax.axis_index("x") * heads * C).astype(jnp.int32).reshape(1)
    kmsg = spread(pack(keys, (beta.T, log_decay.T)))
    v = spread(pack(values))
    q = spread(pack(queries))
    maps = run_keys(starts, base, kmsg)
    zf, zb, total = run_scan(starts, base, v, maps)
    arrived = [
        lax.ppermute(total, "x", [(i, (i + d) % groups) for i in range(groups)]) for d in (1, 2, 3)
    ]
    f = run_queries(q, maps, zf, zb)
    return unpack(spread(run_final(starts, base, f, arrived)))


def solution(mesh):
    fine = Mesh(mesh.devices.reshape(4, 4, 4, 2), ("x", "y", "z", "core"))
    rows = P(("x", "y", "z", "core"), None)
    return jax.shard_map(
        on_device,
        mesh=fine,
        in_specs=(rows,) * 5 + (P(),),
        out_specs=rows,
        check_vma=False,
    )
```

```python
import functools

import jax
import jax.numpy as jnp
from jax import lax
from jax.experimental import pallas as pl
from jax.experimental.pallas import tpu as pltpu
from jax.sharding import Mesh, PartitionSpec as P

D = 128
C = 128
BASE = 16
EXTRA = 16
CUT = 128.0
VMEM_MIB = 50
F32 = jnp.float32
BF16 = jnp.bfloat16
GROUP = ("y", "z", "core")


def split(x):
    hi = x.astype(BF16)
    return hi, (x - hi.astype(F32)).astype(BF16)


def mm(a, b):
    return lax.dot_general(a, b, (((1,), (0,)), ((), ())), preferred_element_type=F32)


def lhs3(pair):
    return jnp.concatenate([pair[0], pair[1], pair[0]], axis=1)


def rhs3(pair):
    return jnp.concatenate([pair[0], pair[0], pair[1]], axis=0)


def dot3(a, b):
    return mm(lhs3(split(a)), rhs3(split(b)))


def beside(x):
    return jnp.concatenate(split(x), axis=1)


def below(x):
    return jnp.concatenate(split(x), axis=0)


def twice(b, axis):
    return jnp.concatenate([b, b], axis=axis)


def widen(ab):
    return jnp.concatenate([ab, ab[:, : ab.shape[1] // 2]], axis=1)


def halves(ab):
    return ab[:, : ab.shape[1] // 2], ab[:, ab.shape[1] // 2 :]


def deepen(hi, lo):
    return jnp.concatenate([hi, hi, lo], axis=0)


def iota(shape, dim):
    return lax.broadcasted_iota(jnp.int32, shape, dim)


def key_kernel(units, starts_ref, base_ref, kmsg_ref, maps_ref):
    step = pl.program_id(0)
    row, col = iota((C, C), 0), iota((C, C), 1)
    extra = kmsg_ref[:, C : C + EXTRA, :].astype(F32)
    beta = jnp.concatenate([extra[u, 0:1] for u in range(units)], axis=0)
    logd = jnp.concatenate([extra[u, 1:2] for u in range(units)], axis=0)
    level = mm(logd.astype(BF16), (row <= col).astype(BF16))
    begin = base_ref[0] + (step * units + iota((units, C), 0)) * C
    place = begin + iota((units, C), 1)
    cuts = jnp.zeros((units, C), F32)
    for n in range(starts_ref.shape[0]):
        at = starts_ref[n]
        cuts += jnp.where((begin < at) & (at <= place), 1.0, 0.0)
    level = level - CUT * cuts
    last = level[:, C - 1 : C]
    carried = jnp.exp(level)
    trail = jnp.exp(last - level)
    gate = jnp.exp(logd)
    inverse_gate = jnp.exp(-logd)
    eye = row == col
    keys = [kmsg_ref[u, :C, :] for u in range(units)]
    turned = [k.T for k in keys]
    gram = [mm(keys[u], turned[u]) for u in range(units)]
    norm = jnp.concatenate(
        [jnp.sum(jnp.where(eye, g, 0.0), axis=0, keepdims=True) for g in gram], axis=0
    )
    scale = 1.0 / jnp.sqrt(norm + 1e-6)
    columns = jnp.concatenate(
        [level, beta * scale, beta, carried * scale, trail * scale], axis=0
    ).T

    def column(which, u):
        return columns[:, which * units + u : which * units + u + 1]

    same = (row // BASE) == (col // BASE)
    systems, compact = [], []
    for u in range(units):
        decay = jnp.exp(-jnp.abs(column(0, u) - level[u : u + 1]))
        weighted = decay * scale[u : u + 1]
        maps_ref[u, 8] = beside(weighted)
        system = jnp.where(row > col, gram[u] * weighted * column(1, u), 0.0)
        systems.append(system)
        inside = jnp.where(same, system, 0.0)
        compact.append(sum(inside[i * BASE : (i + 1) * BASE] for i in range(C // BASE)))
    lane = iota((BASE, C), 1)
    small_row = iota((BASE, C), 0)
    solved = [jnp.where(small_row == lane % BASE, 1.0, 0.0) for u in range(units)]
    first = (lane // BASE) * BASE
    for j in range(BASE - 1):
        top = (j // 8) * 8
        for u in range(units):
            factor = jnp.take_along_axis(compact[u][top:], first[top:] + j, axis=1)
            low = solved[u][top:] - factor * solved[u][j : j + 1]
            solved[u] = jnp.concatenate([solved[u][:top], low], axis=0) if top else low
    full = [
        jnp.where(same, jnp.concatenate([solved[u]] * (C // BASE), axis=0), 0.0)
        for u in range(units)
    ]
    half_row, half_col = iota((C // 2, C), 0), iota((C // 2, C), 1)
    size = BASE
    while size < C:
        pieces = range(C // (2 * size))

        def lower_rows(t):
            return jnp.concatenate([t[(2 * i + 1) * size : (2 * i + 2) * size] for i in pieces], axis=0)

        inside = (half_col // size) == 2 * (half_row // size)
        zero = jnp.zeros((size, C), F32)
        part = [
            dot3(jnp.where(inside, lower_rows(systems[u]), 0.0), full[u]) for u in range(units)
        ]
        for u in range(units):
            rows = [part[u][i * size : (i + 1) * size] for i in pieces]
            spread = jnp.concatenate([block for r in rows for block in (zero, r)], axis=0)
            part[u] = dot3(lower_rows(full[u]), spread)
        for u in range(units):
            t = full[u]
            blocks_of = []
            for i in pieces:
                blocks_of.append(t[2 * i * size : (2 * i + 1) * size])
                blocks_of.append(
                    t[(2 * i + 1) * size : (2 * i + 2) * size] - part[u][i * size : (i + 1) * size]
                )
            full[u] = jnp.concatenate(blocks_of, axis=0)
        size *= 2
    both = [None] * units
    for u in range(units):
        one = slice(u, u + 1)
        y = full[u] * beta[one]
        yt = full[u].T * column(2, u)
        maps_ref[u, 2] = beside(y)
        maps_ref[u, 5] = beside(yt * inverse_gate[one])
        right = jnp.concatenate([y * column(4, u), yt * column(3, u)], axis=1)
        both[u] = mm(twice(turned[u], 1), below(right))
    rests = [None] * units
    for u in range(units):
        one = slice(u, u + 1)
        xt, wt = both[u][:, :C], both[u][:, C:]
        rests[u] = mm(beside(xt * (carried[one] * scale[one])), twice(keys[u], 0))
        maps_ref[u, 1] = beside(xt)
        maps_ref[u, 4] = beside(wt * inverse_gate[one])
        maps_ref[u, 6] = beside(wt.T)
        maps_ref[u, 7] = beside(xt.T)
        rows = jnp.concatenate([carried[one], trail[one], gate[one], jnp.zeros((5, C), F32)], axis=0)
        hi = rows.astype(BF16).astype(F32)
        rows = jnp.concatenate([hi, rows - hi, jnp.zeros((C - 16, C), F32)], axis=0).astype(BF16)
        maps_ref[u, 9] = jnp.concatenate([turned[u], rows], axis=1)
    for u in range(units):
        at = jnp.where(eye, carried[u : u + 1, C - 1 : C], 0.0) - rests[u]
        maps_ref[u, 0] = beside(at)
        maps_ref[u, 3] = beside(at.T)


def is_start(starts_ref, at):
    found = starts_ref[0] == at
    for n in range(1, starts_ref.shape[0]):
        found = found | (starts_ref[n] == at)
    return found


def keep(cut):
    return jnp.where(cut, 0.0, 1.0)


def scan_kernel(
    units, chunks, starts_ref, base_ref, ff_ref, vf_ref, bb_ref, vb_ref,
    zf_ref, zb_ref, total_ref, forward, backward,
):
    step = pl.program_id(0)

    @pl.when(step == 0)
    def _():
        eye = jnp.where(iota((D, D), 0) == iota((D, D), 1), 1.0, 0.0)
        start = jnp.concatenate([jnp.zeros((D, D), F32), eye], axis=1)
        forward[...] = start
        backward[...] = start

    zero = jnp.zeros((D, D), F32)

    def prepare(maps_ref, v_ref, z_ref, u):
        both = mm(maps_ref[u, 1:3].reshape(2 * C, 2 * D), twice(v_ref[u], 0))
        z_ref[u, 2] = beside(both[C:])
        return both[:C]

    def keep_state(z_ref, u, z):
        pair = split(z)
        z_ref[u, 0], z_ref[u, 1] = pair
        return pair

    def beyond(inject):
        return jnp.concatenate([inject, zero], axis=1)

    def keeps(u):
        n = step * units + u
        cut_f = is_start(starts_ref, base_ref[0] + n * C) & (n > 0)
        cut_b = is_start(starts_ref, base_ref[0] + (chunks - n) * C) & (n > 0)
        return keep(cut_f), keep(cut_b)

    inject_f, inject_b = {}, {}

    def ready(u):
        if u < units:
            inject_f[u] = prepare(ff_ref, vf_ref, zf_ref, u)
            inject_b[units - 1 - u] = prepare(bb_ref, vb_ref, zb_ref, units - 1 - u)

    ready(0)
    last = units - 1
    zf, zb = forward[...], backward[...]
    for u in range(units):
        r = last - u
        kept_f, kept_b = keeps(u)
        pair_f = keep_state(zf_ref, u, zf * kept_f)
        pair_b = keep_state(zb_ref, r, zb * kept_b)
        zf = mm(widen(ff_ref[u, 0]), deepen(*pair_f))
        zb = mm(widen(bb_ref[r, 0]), deepen(*pair_b))
        ready(u + 1)
        zf = zf + beyond(inject_f[u])
        zb = zb + beyond(inject_b[r])
    forward[...] = zf
    backward[...] = zb
    total_ref[0] = zf[:, D:]
    total_ref[1] = zf[:, :D]
    total_ref[2] = zb[:, :D]


def query_kernel(units, q_ref, maps_ref, more_ref, zf_ref, zb_ref, f_ref):
    row, col = iota((C, C), 0), iota((C, C), 1)

    def pairs(one, two):
        one_hi, one_lo = halves(one)
        two_hi, two_lo = halves(two)
        return deepen(
            jnp.concatenate([one_hi, two_hi], axis=1), jnp.concatenate([one_lo, two_lo], axis=1)
        )

    every = range(units)
    rows = [more_ref[u, 0, :16, C:].astype(F32) for u in every]
    columns = [(rows[u][:8] + rows[u][8:]).T for u in every]
    scores = [mm(q_ref[u], more_ref[u, 0, :, :C]) for u in every]
    first, second = [None] * units, [None] * units
    for u in every:
        se_hi, se_lo = halves(maps_ref[u, 2])
        score = scores[u] * (se_hi.astype(F32) + se_lo.astype(F32))
        lower = beside(jnp.where(col <= row, score, 0.0))
        upper = beside(jnp.where(col > row, score, 0.0))
        first[u] = mm(widen(lower), pairs(zf_ref[u, 2], maps_ref[u, 0]))
        second[u] = mm(widen(upper), pairs(zb_ref[u, 2], maps_ref[u, 1]))
    third, fourth = [None] * units, [None] * units
    for u in every:
        carried, trail, gate = (columns[u][:, i : i + 1] for i in range(3))
        q = q_ref[u].astype(F32)
        effect_f = carried * q - first[u][:, D:]
        effect_b = gate * (trail * q - second[u][:, D:])
        third[u] = mm(widen(beside(effect_f)), deepen(zf_ref[u, 0], zf_ref[u, 1]))
        fourth[u] = mm(widen(beside(effect_b)), deepen(zb_ref[u, 0], zb_ref[u, 1]))
    for u in every:
        gate = columns[u][:, 2:3]
        total = first[u][:, :D] + gate * second[u][:, :D] + third[u][:, :D] + fourth[u][:, :D]
        f_ref[u, 0] = beside(total)
        hi, lo = split(jnp.concatenate([third[u][:, D:], fourth[u][:, D:]], axis=1))
        f_ref[u, 1] = hi
        f_ref[u, 2] = lo


def final_kernel(units, span, starts_ref, base_ref, f_ref, one_ref, two_ref, three_ref, mixed_ref, state):
    step = pl.program_id(0)

    @pl.when(step == 0)
    def _():
        mine = base_ref[0] // span
        arrived = {1: one_ref, 2: two_ref, 3: three_ref}
        turned = {d: arrived[d][0].T for d in arrived}
        sf = jnp.zeros((D, D), F32)
        sb = jnp.zeros((D, D), F32)
        for d in (1, 2, 3):
            e = 4 - d
            cut = is_start(starts_ref, (mine - e) * span)
            moved = dot3(arrived[e][0], sf * keep(cut)) + arrived[e][1]
            sf = jnp.where(e <= mine, moved, sf)
            cut = is_start(starts_ref, (mine - d + 5) * span)
            moved = dot3(turned[d], sb * keep(cut)) + arrived[d][2]
            sb = jnp.where(d > mine, moved, sb)
        sf = sf * keep(is_start(starts_ref, mine * span))
        sb = sb * keep(is_start(starts_ref, (mine + 1) * span))
        state[...] = beside(jnp.concatenate([sf, sb], axis=0))

    def rows_of(which):
        return f_ref[:, which].reshape(units * C, 2 * D)

    wide = mm(rows_of(1), state[...])
    more = mm(rows_of(2), state[:, :D])
    hi, lo = halves(rows_of(0))
    total = (hi.astype(F32) + lo.astype(F32)) + (wide[:, :D] + wide[:, D:] + more)
    mixed_ref[...] = total.reshape(units, C, D).astype(BF16)


def pack_kernel(src_ref, dst_ref):
    for h in range(dst_ref.shape[0]):
        dst_ref[h] = src_ref[:, h * D : (h + 1) * D]


def pack_extra_kernel(src_ref, beta_ref, decay_ref, dst_ref):
    beta = beta_ref[...].astype(F32)
    decay = decay_ref[...].astype(F32)
    zero = jnp.zeros((EXTRA - 2, C), F32)
    for h in range(dst_ref.shape[0]):
        one = slice(h, h + 1)
        dst_ref[h, :C] = src_ref[:, h * D : (h + 1) * D]
        dst_ref[h, C:] = jnp.concatenate([beta[one], decay[one], zero], axis=0).astype(BF16)


def unpack_kernel(src_ref, dst_ref):
    for h in range(src_ref.shape[0]):
        dst_ref[:, h * D : (h + 1) * D] = src_ref[h]


def blocks(units, *tail, flip=None, group=0):
    back = (0,) * (len(tail) - 1)
    if flip is None:
        return pl.BlockSpec((units,) + tail, lambda i: (i, group) + back)
    return pl.BlockSpec((units,) + tail, lambda i: (flip - 1 - i, group) + back)


SCALARS = [pl.BlockSpec(memory_space=pltpu.SMEM)] * 2


def params(mib=VMEM_MIB):
    return pltpu.CompilerParams(vmem_limit_bytes=mib * 1024 * 1024)


def cost(flops, moved):
    return pl.CostEstimate(flops=flops, bytes_accessed=moved, transcendentals=0)


def pack(array, extra=None, units=16):
    own, width = array.shape
    heads = width // D
    rows = own + (EXTRA if extra is not None else 0)
    return pl.pallas_call(
        pack_kernel if extra is None else pack_extra_kernel,
        grid=(heads // units,),
        in_specs=[pl.BlockSpec((own, units * D), lambda i: (0, i))]
        + ([] if extra is None else [pl.BlockSpec((units, own), lambda i: (i, 0))] * 2),
        out_specs=blocks(units, rows, D),
        out_shape=jax.ShapeDtypeStruct((heads, rows, D), BF16),
        compiler_params=params(60),
        cost_estimate=cost(0, 4_000_000),
        name="pack",
    )(*([array] if extra is None else [array, *extra]))


def unpack(array, units=16):
    heads, own, _ = array.shape
    return pl.pallas_call(
        unpack_kernel,
        grid=(heads // units,),
        in_specs=[blocks(units, own, D)],
        out_specs=pl.BlockSpec((own, units * D), lambda i: (0, i)),
        out_shape=jax.ShapeDtypeStruct((own, heads * D), BF16),
        compiler_params=params(36),
        cost_estimate=cost(0, 4_000_000),
        name="unpack",
    )(array)


def triples(chunks, count=3):
    return jax.ShapeDtypeStruct((chunks, count, C, 2 * D), BF16)


def run_keys(starts, base, kmsg, units=8):
    chunks = kmsg.shape[0]
    return pl.pallas_call(
        functools.partial(key_kernel, units),
        grid=(chunks // units,),
        in_specs=SCALARS + [blocks(units, C + EXTRA, D)],
        out_specs=blocks(units, 10, C, 2 * D),
        out_shape=triples(chunks, 10),
        compiler_params=params(),
        cost_estimate=cost(20_000_000_000, 20_000_000),
        name="key_maps",
    )(starts, base, kmsg)


def run_scan(starts, base, v, maps, units=8):
    chunks = v.shape[0]
    n = chunks // units
    return pl.pallas_call(
        functools.partial(scan_kernel, units, chunks),
        grid=(n,),
        in_specs=SCALARS
        + [blocks(units, 3, C, 2 * D), blocks(units, C, D)]
        + [blocks(units, 3, C, 2 * D, flip=n, group=1), blocks(units, C, D, flip=n)],
        out_specs=[blocks(units, 3, C, 2 * D), blocks(units, 3, C, 2 * D, flip=n)]
        + [pl.BlockSpec((3, D, D), lambda i: (0, 0, 0))],
        out_shape=[triples(chunks)] * 2 + [jax.ShapeDtypeStruct((3, D, D), F32)],
        scratch_shapes=[pltpu.VMEM((D, 2 * D), F32)] * 2,
        compiler_params=params(),
        cost_estimate=cost(20_000_000_000, 20_000_000),
        name="scan",
    )(starts, base, maps, v, maps, v)


def run_queries(q, maps, zf, zb, units=16):
    chunks = q.shape[0]
    return pl.pallas_call(
        functools.partial(query_kernel, units),
        grid=(chunks // units,),
        in_specs=[blocks(units, C, D)]
        + [blocks(units, 3, C, 2 * D, group=2), blocks(units, 1, C, 2 * D, group=9)]
        + [blocks(units, 3, C, 2 * D)] * 2,
        out_specs=blocks(units, 3, C, 2 * D),
        out_shape=triples(chunks),
        compiler_params=params(43),
        cost_estimate=cost(20_000_000_000, 20_000_000),
        name="local_out",
    )(q, maps, maps, zf, zb)


def run_final(starts, base, f, arrived, units=16):
    chunks = f.shape[0]
    whole = pl.BlockSpec((3, D, D), lambda i: (0, 0, 0))
    return pl.pallas_call(
        functools.partial(final_kernel, units, chunks * C),
        grid=(chunks // units,),
        in_specs=SCALARS + [blocks(units, 3, C, 2 * D)] + [whole] * 3,
        out_specs=blocks(units, C, D),
        out_shape=jax.ShapeDtypeStruct((chunks, C, D), BF16),
        scratch_shapes=[pltpu.VMEM((2 * D, 2 * D), BF16)],
        compiler_params=params(43),
        cost_estimate=cost(2_000_000_000, 10_000_000),
        name="final",
    )(starts, base, f, *arrived)


def spread(array):
    return lax.all_to_all(array, GROUP, split_axis=0, concat_axis=0, tiled=True)


def on_device(queries, keys, values, beta, log_decay, seg_lengths):
    heads = queries.shape[1] // D
    groups = lax.axis_size("x")
    order = jnp.arange(seg_lengths.shape[0])
    starts = jnp.sum(jnp.where(order[None, :] < order[:, None], seg_lengths[None, :], 0), axis=1)
    starts = starts.astype(jnp.int32)
    base = (lax.axis_index("x") * heads * C).astype(jnp.int32).reshape(1)
    kmsg = spread(pack(keys, (beta.T, log_decay.T)))
    v = spread(pack(values))
    q = spread(pack(queries))
    maps = run_keys(starts, base, kmsg)
    zf, zb, total = run_scan(starts, base, v, maps)
    arrived = [
        lax.ppermute(total, "x", [(i, (i + d) % groups) for i in range(groups)]) for d in (1, 2, 3)
    ]
    f = run_queries(q, maps, zf, zb)
    return unpack(spread(run_final(starts, base, f, arrived)))


def solution(mesh):
    fine = Mesh(mesh.devices.reshape(4, 4, 4, 2), ("x", "y", "z", "core"))
    rows = P(("x", "y", "z", "core"), None)
    return jax.shard_map(
        on_device,
        mesh=fine,
        in_specs=(rows,) * 5 + (P(),),
        out_specs=rows,
        check_vma=False,
    )
```

```python
import functools

import jax
import jax.numpy as jnp
from jax import lax
from jax.experimental import pallas as pl
from jax.experimental.pallas import tpu as pltpu
from jax.sharding import Mesh, PartitionSpec as P

D = 128
C = 128
BASE = 16
EXTRA = 16
CUT = 128.0
VMEM_MIB = 50
F32 = jnp.float32
BF16 = jnp.bfloat16
GROUP = ("y", "z", "core")


def split(x):
    hi = x.astype(BF16)
    return hi, (x - hi.astype(F32)).astype(BF16)


def mm(a, b):
    return lax.dot_general(a, b, (((1,), (0,)), ((), ())), preferred_element_type=F32)


def lhs3(pair):
    return jnp.concatenate([pair[0], pair[1], pair[0]], axis=1)


def rhs3(pair):
    return jnp.concatenate([pair[0], pair[0], pair[1]], axis=0)


def dot3(a, b):
    return mm(lhs3(split(a)), rhs3(split(b)))


def beside(x):
    return jnp.concatenate(split(x), axis=1)


def below(x):
    return jnp.concatenate(split(x), axis=0)


def twice(b, axis):
    return jnp.concatenate([b, b], axis=axis)


def widen(ab):
    return jnp.concatenate([ab, ab[:, : ab.shape[1] // 2]], axis=1)


def halves(ab):
    return ab[:, : ab.shape[1] // 2], ab[:, ab.shape[1] // 2 :]


def deepen(hi, lo):
    return jnp.concatenate([hi, hi, lo], axis=0)


def iota(shape, dim):
    return lax.broadcasted_iota(jnp.int32, shape, dim)


def key_kernel(units, starts_ref, base_ref, kmsg_ref, maps_ref):
    step = pl.program_id(0)
    row, col = iota((C, C), 0), iota((C, C), 1)
    extra = kmsg_ref[:, C : C + EXTRA, :].astype(F32)
    beta = jnp.concatenate([extra[u, 0:1] for u in range(units)], axis=0)
    logd = jnp.concatenate([extra[u, 1:2] for u in range(units)], axis=0)
    level = mm(logd.astype(BF16), (row <= col).astype(BF16))
    begin = base_ref[0] + (step * units + iota((units, C), 0)) * C
    place = begin + iota((units, C), 1)
    cuts = jnp.zeros((units, C), F32)
    for n in range(starts_ref.shape[0]):
        at = starts_ref[n]
        cuts += jnp.where((begin < at) & (at <= place), 1.0, 0.0)
    level = level - CUT * cuts
    last = level[:, C - 1 : C]
    carried = jnp.exp(level)
    trail = jnp.exp(last - level)
    gate = jnp.exp(logd)
    inverse_gate = jnp.exp(-logd)
    eye = row == col
    keys = [kmsg_ref[u, :C, :] for u in range(units)]
    turned = [k.T for k in keys]
    gram = [mm(keys[u], turned[u]) for u in range(units)]
    norm = jnp.concatenate(
        [jnp.sum(jnp.where(eye, g, 0.0), axis=0, keepdims=True) for g in gram], axis=0
    )
    scale = 1.0 / jnp.sqrt(norm + 1e-6)
    columns = jnp.concatenate(
        [level, beta * scale, beta, carried * scale, trail * scale], axis=0
    ).T

    def column(which, u):
        return columns[:, which * units + u : which * units + u + 1]

    same = (row // BASE) == (col // BASE)
    systems, compact = [], []
    for u in range(units):
        decay = jnp.exp(-jnp.abs(column(0, u) - level[u : u + 1]))
        weighted = decay * scale[u : u + 1]
        maps_ref[u, 8] = beside(weighted)
        system = jnp.where(row > col, gram[u] * weighted * column(1, u), 0.0)
        systems.append(system)
        inside = jnp.where(same, system, 0.0)
        compact.append(sum(inside[i * BASE : (i + 1) * BASE] for i in range(C // BASE)))
    lane = iota((BASE, C), 1)
    small_row = iota((BASE, C), 0)
    solved = [jnp.where(small_row == lane % BASE, 1.0, 0.0) for u in range(units)]
    first = (lane // BASE) * BASE
    for j in range(BASE - 1):
        top = (j // 8) * 8
        for u in range(units):
            factor = jnp.take_along_axis(compact[u][top:], first[top:] + j, axis=1)
            low = solved[u][top:] - factor * solved[u][j : j + 1]
            solved[u] = jnp.concatenate([solved[u][:top], low], axis=0) if top else low
    full = [
        jnp.where(same, jnp.concatenate([solved[u]] * (C // BASE), axis=0), 0.0)
        for u in range(units)
    ]
    half_row, half_col = iota((C // 2, C), 0), iota((C // 2, C), 1)
    size = BASE
    while size < C:
        pieces = range(C // (2 * size))

        def lower_rows(t):
            return jnp.concatenate([t[(2 * i + 1) * size : (2 * i + 2) * size] for i in pieces], axis=0)

        inside = (half_col // size) == 2 * (half_row // size)
        zero = jnp.zeros((size, C), F32)
        part = [
            dot3(jnp.where(inside, lower_rows(systems[u]), 0.0), full[u]) for u in range(units)
        ]
        for u in range(units):
            rows = [part[u][i * size : (i + 1) * size] for i in pieces]
            spread = jnp.concatenate([block for r in rows for block in (zero, r)], axis=0)
            part[u] = dot3(lower_rows(full[u]), spread)
        for u in range(units):
            t = full[u]
            blocks_of = []
            for i in pieces:
                blocks_of.append(t[2 * i * size : (2 * i + 1) * size])
                blocks_of.append(
                    t[(2 * i + 1) * size : (2 * i + 2) * size] - part[u][i * size : (i + 1) * size]
                )
            full[u] = jnp.concatenate(blocks_of, axis=0)
        size *= 2
    both = [None] * units
    for u in range(units):
        one = slice(u, u + 1)
        y = full[u] * beta[one]
        yt = full[u].T * column(2, u)
        maps_ref[u, 2] = beside(y)
        maps_ref[u, 5] = beside(yt * inverse_gate[one])
        right = jnp.concatenate([y * column(4, u), yt * column(3, u)], axis=1)
        both[u] = mm(twice(turned[u], 1), below(right))
    rests = [None] * units
    for u in range(units):
        one = slice(u, u + 1)
        xt, wt = both[u][:, :C], both[u][:, C:]
        rests[u] = mm(beside(xt * (carried[one] * scale[one])), twice(keys[u], 0))
        maps_ref[u, 1] = beside(xt)
        maps_ref[u, 4] = beside(wt * inverse_gate[one])
        maps_ref[u, 6] = beside(wt.T)
        maps_ref[u, 7] = beside(xt.T)
        rows = jnp.concatenate([carried[one], trail[one], gate[one], jnp.zeros((5, C), F32)], axis=0)
        hi = rows.astype(BF16).astype(F32)
        rows = jnp.concatenate([hi, rows - hi, jnp.zeros((C - 16, C), F32)], axis=0).astype(BF16)
        maps_ref[u, 9] = jnp.concatenate([turned[u], rows], axis=1)
    for u in range(units):
        at = jnp.where(eye, carried[u : u + 1, C - 1 : C], 0.0) - rests[u]
        maps_ref[u, 0] = beside(at)
        maps_ref[u, 3] = beside(at.T)


def is_start(starts_ref, at):
    found = starts_ref[0] == at
    for n in range(1, starts_ref.shape[0]):
        found = found | (starts_ref[n] == at)
    return found


def keep(cut):
    return jnp.where(cut, 0.0, 1.0)


def scan_kernel(
    units, chunks, starts_ref, base_ref, ff_ref, vf_ref, bb_ref, vb_ref,
    zf_ref, zb_ref, one_ref, two_ref, three_ref, forward, backward,
):
    step = pl.program_id(0)

    @pl.when(step == 0)
    def _():
        eye = jnp.where(iota((D, D), 0) == iota((D, D), 1), 1.0, 0.0)
        start = jnp.concatenate([jnp.zeros((D, D), F32), eye], axis=1)
        forward[...] = start
        backward[...] = start

    zero = jnp.zeros((D, D), F32)

    def prepare(maps_ref, v_ref, z_ref, u):
        both = mm(maps_ref[u, 1:3].reshape(2 * C, 2 * D), twice(v_ref[u], 0))
        z_ref[u, 2] = beside(both[C:])
        return both[:C]

    def keep_state(z_ref, u, z):
        pair = split(z)
        z_ref[u, 0], z_ref[u, 1] = pair
        return pair

    def beyond(inject):
        return jnp.concatenate([inject, zero], axis=1)

    def keeps(u):
        n = step * units + u
        cut_f = is_start(starts_ref, base_ref[0] + n * C) & (n > 0)
        cut_b = is_start(starts_ref, base_ref[0] + (chunks - n) * C) & (n > 0)
        return keep(cut_f), keep(cut_b)

    inject_f, inject_b = {}, {}

    def ready(u):
        if u < units:
            inject_f[u] = prepare(ff_ref, vf_ref, zf_ref, u)
            inject_b[units - 1 - u] = prepare(bb_ref, vb_ref, zb_ref, units - 1 - u)

    ready(0)
    last = units - 1
    zf, zb = forward[...], backward[...]
    for u in range(units):
        r = last - u
        kept_f, kept_b = keeps(u)
        pair_f = keep_state(zf_ref, u, zf * kept_f)
        pair_b = keep_state(zb_ref, r, zb * kept_b)
        zf = mm(widen(ff_ref[u, 0]), deepen(*pair_f))
        zb = mm(widen(bb_ref[r, 0]), deepen(*pair_b))
        ready(u + 1)
        zf = zf + beyond(inject_f[u])
        zb = zb + beyond(inject_b[r])
    forward[...] = zf
    backward[...] = zb
    mine = base_ref[0] // (chunks * C)
    for d, total_ref in ((1, one_ref), (2, two_ref), (3, three_ref)):
        total_ref[0] = zf[:, D:]
        total_ref[1] = jnp.where(mine + d < 4, zf[:, :D], zb[:, :D])


def query_kernel(units, q_ref, maps_ref, more_ref, zf_ref, zb_ref, f_ref):
    row, col = iota((C, C), 0), iota((C, C), 1)

    def pairs(one, two):
        one_hi, one_lo = halves(one)
        two_hi, two_lo = halves(two)
        return deepen(
            jnp.concatenate([one_hi, two_hi], axis=1), jnp.concatenate([one_lo, two_lo], axis=1)
        )

    every = range(units)
    rows = [more_ref[u, 0, :16, C:].astype(F32) for u in every]
    columns = [(rows[u][:8] + rows[u][8:]).T for u in every]
    scores = [mm(q_ref[u], more_ref[u, 0, :, :C]) for u in every]
    first, second = [None] * units, [None] * units
    for u in every:
        se_hi, se_lo = halves(maps_ref[u, 2])
        score = scores[u] * (se_hi.astype(F32) + se_lo.astype(F32))
        lower = beside(jnp.where(col <= row, score, 0.0))
        upper = beside(jnp.where(col > row, score, 0.0))
        first[u] = mm(widen(lower), pairs(zf_ref[u, 2], maps_ref[u, 0]))
        second[u] = mm(widen(upper), pairs(zb_ref[u, 2], maps_ref[u, 1]))
    third, fourth = [None] * units, [None] * units
    for u in every:
        carried, trail, gate = (columns[u][:, i : i + 1] for i in range(3))
        q = q_ref[u].astype(F32)
        effect_f = carried * q - first[u][:, D:]
        effect_b = gate * (trail * q - second[u][:, D:])
        third[u] = mm(widen(beside(effect_f)), deepen(zf_ref[u, 0], zf_ref[u, 1]))
        fourth[u] = mm(widen(beside(effect_b)), deepen(zb_ref[u, 0], zb_ref[u, 1]))
    for u in every:
        gate = columns[u][:, 2:3]
        total = first[u][:, :D] + gate * second[u][:, :D] + third[u][:, :D] + fourth[u][:, :D]
        f_ref[u, 0] = beside(total)
        hi, lo = split(jnp.concatenate([third[u][:, D:], fourth[u][:, D:]], axis=1))
        f_ref[u, 1] = hi
        f_ref[u, 2] = lo


def final_kernel(units, span, starts_ref, base_ref, f_ref, one_ref, two_ref, three_ref, mixed_ref, state):
    step = pl.program_id(0)

    @pl.when(step == 0)
    def _():
        mine = base_ref[0] // span
        arrived = {1: one_ref, 2: two_ref, 3: three_ref}
        turned = {d: arrived[d][0].T for d in arrived}
        sf = jnp.zeros((D, D), F32)
        sb = jnp.zeros((D, D), F32)
        for d in (1, 2, 3):
            e = 4 - d
            cut = is_start(starts_ref, (mine - e) * span)
            moved = dot3(arrived[e][0], sf * keep(cut)) + arrived[e][1]
            sf = jnp.where(e <= mine, moved, sf)
            cut = is_start(starts_ref, (mine - d + 5) * span)
            moved = dot3(turned[d], sb * keep(cut)) + arrived[d][1]
            sb = jnp.where(d > mine, moved, sb)
        sf = sf * keep(is_start(starts_ref, mine * span))
        sb = sb * keep(is_start(starts_ref, (mine + 1) * span))
        state[...] = beside(jnp.concatenate([sf, sb], axis=0))

    def rows_of(which):
        return f_ref[:, which].reshape(units * C, 2 * D)

    wide = mm(rows_of(1), state[...])
    more = mm(rows_of(2), state[:, :D])
    hi, lo = halves(rows_of(0))
    total = (hi.astype(F32) + lo.astype(F32)) + (wide[:, :D] + wide[:, D:] + more)
    mixed_ref[...] = total.reshape(units, C, D).astype(BF16)


def pack_kernel(src_ref, dst_ref):
    for h in range(dst_ref.shape[0]):
        dst_ref[h] = src_ref[:, h * D : (h + 1) * D]


def pack_extra_kernel(src_ref, beta_ref, decay_ref, dst_ref):
    beta = beta_ref[...].astype(F32)
    decay = decay_ref[...].astype(F32)
    zero = jnp.zeros((EXTRA - 2, C), F32)
    for h in range(dst_ref.shape[0]):
        one = slice(h, h + 1)
        dst_ref[h, :C] = src_ref[:, h * D : (h + 1) * D]
        dst_ref[h, C:] = jnp.concatenate([beta[one], decay[one], zero], axis=0).astype(BF16)


def unpack_kernel(src_ref, dst_ref):
    for h in range(src_ref.shape[0]):
        dst_ref[:, h * D : (h + 1) * D] = src_ref[h]


def blocks(units, *tail, flip=None, group=0):
    back = (0,) * (len(tail) - 1)
    if flip is None:
        return pl.BlockSpec((units,) + tail, lambda i: (i, group) + back)
    return pl.BlockSpec((units,) + tail, lambda i: (flip - 1 - i, group) + back)


SCALARS = [pl.BlockSpec(memory_space=pltpu.SMEM)] * 2


def params(mib=VMEM_MIB):
    return pltpu.CompilerParams(vmem_limit_bytes=mib * 1024 * 1024)


def cost(flops, moved):
    return pl.CostEstimate(flops=flops, bytes_accessed=moved, transcendentals=0)


def pack(array, extra=None, units=16):
    own, width = array.shape
    heads = width // D
    rows = own + (EXTRA if extra is not None else 0)
    return pl.pallas_call(
        pack_kernel if extra is None else pack_extra_kernel,
        grid=(heads // units,),
        in_specs=[pl.BlockSpec((own, units * D), lambda i: (0, i))]
        + ([] if extra is None else [pl.BlockSpec((units, own), lambda i: (i, 0))] * 2),
        out_specs=blocks(units, rows, D),
        out_shape=jax.ShapeDtypeStruct((heads, rows, D), BF16),
        compiler_params=params(60),
        cost_estimate=cost(0, 4_000_000),
        name="pack",
    )(*([array] if extra is None else [array, *extra]))


def unpack(array, units=16):
    heads, own, _ = array.shape
    return pl.pallas_call(
        unpack_kernel,
        grid=(heads // units,),
        in_specs=[blocks(units, own, D)],
        out_specs=pl.BlockSpec((own, units * D), lambda i: (0, i)),
        out_shape=jax.ShapeDtypeStruct((own, heads * D), BF16),
        compiler_params=params(36),
        cost_estimate=cost(0, 4_000_000),
        name="unpack",
    )(array)


def triples(chunks, count=3):
    return jax.ShapeDtypeStruct((chunks, count, C, 2 * D), BF16)


def run_keys(starts, base, kmsg, units=8):
    chunks = kmsg.shape[0]
    return pl.pallas_call(
        functools.partial(key_kernel, units),
        grid=(chunks // units,),
        in_specs=SCALARS + [blocks(units, C + EXTRA, D)],
        out_specs=blocks(units, 10, C, 2 * D),
        out_shape=triples(chunks, 10),
        compiler_params=params(),
        cost_estimate=cost(20_000_000_000, 20_000_000),
        name="key_maps",
    )(starts, base, kmsg)


def run_scan(starts, base, v, maps, units=8):
    chunks = v.shape[0]
    n = chunks // units
    return pl.pallas_call(
        functools.partial(scan_kernel, units, chunks),
        grid=(n,),
        in_specs=SCALARS
        + [blocks(units, 3, C, 2 * D), blocks(units, C, D)]
        + [blocks(units, 3, C, 2 * D, flip=n, group=1), blocks(units, C, D, flip=n)],
        out_specs=[blocks(units, 3, C, 2 * D), blocks(units, 3, C, 2 * D, flip=n)]
        + [pl.BlockSpec((2, D, D), lambda i: (0, 0, 0))] * 3,
        out_shape=[triples(chunks)] * 2 + [jax.ShapeDtypeStruct((2, D, D), F32)] * 3,
        scratch_shapes=[pltpu.VMEM((D, 2 * D), F32)] * 2,
        compiler_params=params(),
        cost_estimate=cost(20_000_000_000, 20_000_000),
        name="scan",
    )(starts, base, maps, v, maps, v)


def run_queries(q, maps, zf, zb, units=16):
    chunks = q.shape[0]
    return pl.pallas_call(
        functools.partial(query_kernel, units),
        grid=(chunks // units,),
        in_specs=[blocks(units, C, D)]
        + [blocks(units, 3, C, 2 * D, group=2), blocks(units, 1, C, 2 * D, group=9)]
        + [blocks(units, 3, C, 2 * D)] * 2,
        out_specs=blocks(units, 3, C, 2 * D),
        out_shape=triples(chunks),
        compiler_params=params(43),
        cost_estimate=cost(20_000_000_000, 20_000_000),
        name="local_out",
    )(q, maps, maps, zf, zb)


def run_final(starts, base, f, arrived, units=16):
    chunks = f.shape[0]
    whole = pl.BlockSpec((2, D, D), lambda i: (0, 0, 0))
    return pl.pallas_call(
        functools.partial(final_kernel, units, chunks * C),
        grid=(chunks // units,),
        in_specs=SCALARS + [blocks(units, 3, C, 2 * D)] + [whole] * 3,
        out_specs=blocks(units, C, D),
        out_shape=jax.ShapeDtypeStruct((chunks, C, D), BF16),
        scratch_shapes=[pltpu.VMEM((2 * D, 2 * D), BF16)],
        compiler_params=params(43),
        cost_estimate=cost(2_000_000_000, 10_000_000),
        name="final",
    )(starts, base, f, *arrived)


def spread(array):
    return lax.all_to_all(array, GROUP, split_axis=0, concat_axis=0, tiled=True)


def on_device(queries, keys, values, beta, log_decay, seg_lengths):
    heads = queries.shape[1] // D
    groups = lax.axis_size("x")
    order = jnp.arange(seg_lengths.shape[0])
    starts = jnp.sum(jnp.where(order[None, :] < order[:, None], seg_lengths[None, :], 0), axis=1)
    starts = starts.astype(jnp.int32)
    base = (lax.axis_index("x") * heads * C).astype(jnp.int32).reshape(1)
    kmsg = spread(pack(keys, (beta.T, log_decay.T)))
    v = spread(pack(values))
    q = spread(pack(queries))
    maps = run_keys(starts, base, kmsg)
    zf, zb, *totals = run_scan(starts, base, v, maps)
    arrived = [
        lax.ppermute(totals[d - 1], "x", [(i, (i + d) % groups) for i in range(groups)])
        for d in (1, 2, 3)
    ]
    f = run_queries(q, maps, zf, zb)
    return unpack(spread(run_final(starts, base, f, arrived)))


def solution(mesh):
    fine = Mesh(mesh.devices.reshape(4, 4, 4, 2), ("x", "y", "z", "core"))
    rows = P(("x", "y", "z", "core"), None)
    return jax.shard_map(
        on_device,
        mesh=fine,
        in_specs=(rows,) * 5 + (P(),),
        out_specs=rows,
        check_vma=False,
    )
```
